512 devices in a mesh: ctx: 32 (over x, y), head: 16 (over z, core).
Axes of the slice: x: 4, y: 8, z: 8, core: 2. Of those that a mesh axis runs over, the one named last changes fastest.
Arguments:
- light_query: bfloat16 [65536, 2048], P(('ctx', 'head')), may hold values from -6 to 6
- light_key: bfloat16 [65536, 2048], P(('ctx', 'head')), may hold values from -6 to 6
- light_value: bfloat16 [65536, 2048], P(('ctx', 'head')), may hold values from -6 to 6
- soft_query: bfloat16 [65536, 2048], P(('ctx', 'head')), may hold values from -52 to 52
- soft_key: bfloat16 [65536, 2048], P(('ctx', 'head')), may hold values from -6 to 6
- upstream: bfloat16 [65536, 2048], P(('ctx', 'head')), may hold values from -6 to 6
- decays: bfloat16 [65536, 32], P(('ctx', 'head')), may hold values from 0 to 1
- block_mask: int32 [512, 16], P('ctx'), may hold values from 0 to 1, as said below
Outputs:
- grad_light_query: bfloat16 [65536, 2048], P(('ctx', 'head'))
- grad_light_key: bfloat16 [65536, 2048], P(('ctx', 'head'))
- grad_light_value: bfloat16 [65536, 2048], P(('ctx', 'head'))
The draws below stay inside these ranges and needn't reach their ends.
Inputs may be any that keep to these rules, and one draw needn't show every extreme that they name: `block_mask`: in each query block, the flag of its own block within the span is 1 and flags of later blocks are 0; earlier blocks are 0 or 1.
All inputs are finite; a program needn't handle non-finite values.
Results may differ from the reference program's by a relative error of at most 0.0057.
Values may be sent and summed in bfloat16 or wider, within the bound.
A program may use at most 64 MiB of HBM per device.

```python
import math
import jax
import jax.numpy as jnp
from jax import lax

HD = 64
HEADS = 32
BLOCK = 128
SPAN = 2048
SEQ = 65536
N_CTX = 32


def soft_pair(key):
    base = jax.random.fold_in(key, 7117)
    key_seed, query_seed = jax.random.split(base, 2)
    shape = (SEQ, HEADS * HD)
    keys = jnp.clip(jax.random.normal(key_seed, shape, jnp.float32), -6.0, 6.0)
    queries = jnp.clip(jax.random.normal(query_seed, shape, jnp.float32), -6.0, 6.0)
    return (queries, keys)


def draw_soft_query(key, part):
    return soft_pair(key)[0].astype(jnp.bfloat16)


def draw_soft_key(key, part):
    return soft_pair(key)[1].astype(jnp.bfloat16)


def draw_decays(key, part):
    seeds = jax.random.split(jax.random.fold_in(key, 311), 6)
    cutoff = 5
    fast = jax.random.randint(seeds[0], (HEADS,), 0, 10) < cutoff
    fast_rate = jnp.exp(jax.random.uniform(seeds[1], (HEADS,), jnp.float32, math.log(1.0 / 50.0), math.log(1.0 / 30.0)))
    slow_rate = 0.3 / SEQ * jax.random.uniform(seeds[2], (HEADS,), jnp.float32, 0.5, 1.0)
    baseline_decay_rate = jnp.where(fast, fast_rate, slow_rate)
    multiplier_value = jnp.exp(jax.random.uniform(seeds[3], (SEQ, HEADS), jnp.float32, math.log(0.5), math.log(2.0)))
    spots = jax.random.randint(seeds[4], (3, HEADS), 0, SEQ)
    spike_magnitude = -jnp.log(1.0 - jax.random.uniform(seeds[5], (3, HEADS), jnp.float32, 0.2, 0.4))
    matched_entries = jnp.arange(SEQ)[:, None, None] == spots[None]
    spike_positions = jnp.sum(jnp.where(matched_entries, spike_magnitude[None], 0.0), axis=1)
    return (baseline_decay_rate[None, :] * multiplier_value + spike_positions).astype(jnp.bfloat16)


def draw_block_mask(key, part):
    blocks = SPAN // BLOCK
    flags = jax.random.randint(jax.random.fold_in(key, 53), (SEQ // BLOCK, blocks), 0, 2)
    own = (jnp.arange(SEQ // BLOCK) % blocks)[:, None]
    column = jnp.arange(blocks)[None, :]
    return jnp.where(column == own, 1, jnp.where(column < own, flags, 0)).astype(jnp.int32)


def shard_levels(own_key, extent, shards, least, high):
    factor_of, own = 1.0, jax.random.fold_in(own_key, 6)
    for dim, parts in shards:
        steps = jnp.exp(jax.random.uniform(jax.random.fold_in(own, dim), (parts,), jnp.float32, least / len(shards), high / len(shards)))
        factor_of = factor_of * jnp.repeat(steps, extent[dim] // parts).reshape([-1 if axis == dim else 1 for axis in range(len(extent))])
    return factor_of


def scatter_about(rng, shape, scale, most, pieces=(), held_as=jnp.bfloat16):
    factor_of = shard_levels(rng, shape, pieces, -0.22, 0.18) if pieces else 1.0
    result = jax.random.normal(rng, shape, jnp.float32) * scale * factor_of
    return jnp.minimum(jnp.maximum(result, -most), most).astype(held_as)


def setup_inputs(seed: int = 0) -> dict:
    arg_keys = jax.random.split(jax.random.key(seed), 9)
    light_query = scatter_about(arg_keys[0], (SEQ, HEADS * HD), 1.0, 6.0, ((0, 512),))
    light_key = scatter_about(arg_keys[1], (SEQ, HEADS * HD), 1.0, 6.0, ((0, 512),))
    light_value = scatter_about(arg_keys[2], (SEQ, HEADS * HD), 1.0, 6.0, ((0, 512),))
    soft_query = draw_soft_query(jax.random.fold_in(arg_keys[8], 71), 0)
    soft_key = draw_soft_key(jax.random.fold_in(arg_keys[8], 71), 0)
    upstream = scatter_about(arg_keys[5], (SEQ, HEADS * HD), 1.0, 6.0, ((0, 512),))
    decays = draw_decays(jax.random.fold_in(arg_keys[8], 71), 0)
    block_mask = draw_block_mask(jax.random.fold_in(arg_keys[8], 71), 0)
    return dict(light_query=light_query, light_key=light_key, light_value=light_value, soft_query=soft_query, soft_key=soft_key, upstream=upstream, decays=decays, block_mask=block_mask)


HIGH = lax.Precision.HIGHEST

def combine_pairs(earlier, later):
    return (earlier[0] * later[0], later[0][:, None, None] * earlier[1] + later[1])

def span_tables(decay_rows):
    levels = jnp.cumsum(decay_rows.astype(jnp.float32).T, axis=1)
    count = levels.shape[1]
    places = jnp.arange(count)
    lower = places[None, :] <= places[:, None]
    spread = levels[:, None, :] - levels[:, :, None]
    weights = jnp.where(lower[None], jnp.exp(jnp.minimum(spread, 0.0)), 0.0)
    finals = levels[:, -1]
    entries = jnp.exp(-levels).T
    leaving = jnp.exp(levels - finals[:, None]).T
    return (weights, entries, leaving, jnp.exp(-finals))

def allowed_pairs(flags, count):
    places = jnp.arange(count)
    expanded = jnp.repeat(jnp.repeat(flags, BLOCK, axis=0), BLOCK, axis=1)
    return (expanded == 1) & (places[None, :] <= places[:, None])

def mixing(form, left, right):
    return jnp.einsum(form, left.astype(jnp.float32), right.astype(jnp.float32), precision=HIGH)

def exact(form, left, right):
    return jnp.einsum(form, left, right, precision=HIGH)

def summary_of(light_key, light_value, decay_blocks):
    weights, entries, leaving, running_totals = jax.vmap(span_tables)(decay_blocks)
    block_sums = exact('nshi,nshj->nhij', light_key.astype(jnp.float32) * leaving[..., None], light_value.astype(jnp.float32))
    return (running_totals, block_sums)

def middle_pass(light_query, soft_query, soft_key, upstream, decay_blocks, flags):
    weights, entries, leaving, running_totals = jax.vmap(span_tables)(decay_blocks)
    head_width = soft_query.shape[2]
    root = 1.0 / math.sqrt(head_width)
    allowed = allowed_pairs(flags, soft_query.shape[0])

    def one_head(items):
        query_per_head, key_h, cotan_h = items
        scores = mixing('td,sd->ts', query_per_head, key_h) * root
        scores = jnp.where(allowed, scores, -jnp.inf)
        highest = lax.optimization_barrier(jnp.max(scores, axis=-1, keepdims=True))
        powers = jnp.exp(scores - highest)
        probs = powers / lax.optimization_barrier(jnp.sum(powers, axis=-1, keepdims=True))
        probs_low = probs.astype(jnp.bfloat16)
        return mixing('ts,td->sd', probs_low, cotan_h).astype(jnp.bfloat16)
    lit_grad = lax.map(one_head, (jnp.transpose(soft_query, (1, 0, 2)), jnp.transpose(soft_key, (1, 0, 2)), jnp.transpose(upstream, (1, 0, 2))))
    lit_grad = jnp.transpose(lit_grad, (1, 0, 2)).reshape(light_query.shape)
    reach = exact('nthi,nthj->nhij', light_query.astype(jnp.float32) * entries[..., None], lit_grad.astype(jnp.float32))
    return (lit_grad, reach)

def last_pass(light_query, light_key, light_value, lit_grad, decay_blocks, state_in, reach_in):
    weights, entries, leaving, running_totals = jax.vmap(span_tables)(decay_blocks)
    head_width = light_query.shape[3]
    scale = 1.0 / (head_width * math.sqrt(head_width))
    mixed = (mixing('nthd,nshd->nhts', light_query, light_key) * weights).astype(jnp.bfloat16)
    back = (mixing('nthd,nshd->nhts', lit_grad, light_value) * weights).astype(jnp.bfloat16)
    grad_query = scale * (mixing('nhts,nshd->nthd', back, light_key) + entries[..., None] * exact('nthj,nhij->nthi', lit_grad.astype(jnp.float32), state_in))
    grad_key = scale * (mixing('nhts,nthd->nshd', back, light_query) + leaving[..., None] * exact('nshj,nhij->nshi', light_value.astype(jnp.float32), reach_in))
    grad_value = scale * (mixing('nhts,nthd->nshd', mixed, lit_grad) + leaving[..., None] * exact('nshi,nhij->nshj', light_key.astype(jnp.float32), reach_in))
    return (grad_query.astype(jnp.bfloat16), grad_key.astype(jnp.bfloat16), grad_value.astype(jnp.bfloat16))

def reference(light_query, light_key, light_value, soft_query, soft_key, upstream, decays, block_mask):
    blocks = SPAN // BLOCK
    shaped = (N_CTX, blocks, BLOCK, HEADS, HD)
    spanned = (N_CTX, SPAN, HEADS, HD)
    query_one = light_query.reshape(shaped)
    key_one = light_key.reshape(shaped)
    value_one = light_value.reshape(shaped)
    query_two = soft_query.reshape(spanned)
    key_two = soft_key.reshape(spanned)
    cotan = upstream.reshape(spanned)
    decay_all = decays.reshape(N_CTX, blocks, BLOCK, HEADS)
    flag_all = block_mask.reshape(N_CTX, blocks, blocks)

    def one_summary(items):
        return summary_of(items[0], items[1], items[2])
    running_totals, block_sums = lax.map(one_summary, (key_one, value_one, decay_all))
    running_totals = running_totals.reshape(N_CTX * blocks, HEADS)
    block_sums = block_sums.reshape(N_CTX * blocks, HEADS, HD, HD)
    identity = (jnp.ones((HEADS,), jnp.float32), jnp.zeros((HEADS, HD, HD), jnp.float32))

    def carry_step(carried, item):
        return (combine_pairs(carried, item), carried)
    _, prefix = lax.scan(carry_step, identity, (running_totals, block_sums))
    states = prefix[1].reshape(N_CTX, blocks, HEADS, HD, HD)

    def one_middle(items):
        return middle_pass(*items)
    lit_grads, reaches = lax.map(one_middle, (query_one, query_two, key_two, cotan, decay_all, flag_all))
    _, suffix = lax.scan(carry_step, identity, (running_totals, reaches.reshape(N_CTX * blocks, HEADS, HD, HD)), reverse=True)
    reach_ins = suffix[1].reshape(N_CTX, blocks, HEADS, HD, HD)

    def one_last(items):
        return last_pass(*items)
    grad_q_one, grad_k_one, grad_v_one = lax.map(one_last, (query_one, key_one, value_one, lit_grads, decay_all, states, reach_ins))
    flat = (SEQ, HEADS * HD)
    return (grad_q_one.reshape(flat), grad_k_one.reshape(flat), grad_v_one.reshape(flat))
```

```python
import functools
import math

import jax
import jax.numpy as jnp
from jax import lax
from jax.experimental import pallas as pl
from jax.experimental.pallas import tpu as pltpu
from jax.sharding import PartitionSpec as P

T = 128
W = 128
HD = 64
MSG = 80
LOW = -1e30
F32 = jnp.float32
BF16 = jnp.bfloat16
MESH = pl.DeviceIdType.MESH


def dot(a, b, ca=1, cb=0):
    return lax.dot_general(a, b, (((ca,), (cb,)), ((), ())), preferred_element_type=F32)


def dot_split(a, b, ca=1, cb=0):
    high = a.astype(BF16)
    low = (a - high.astype(F32)).astype(BF16)
    return dot(high, b, ca, cb) + dot(low, b, ca, cb)


def halves(x):
    first = lax.broadcasted_iota(jnp.int32, x.shape, 1) < HD
    zero = jnp.zeros_like(x)
    return jnp.concatenate([jnp.where(first, x, zero), jnp.where(first, zero, x)], axis=0)


def fold(x):
    first = lax.broadcasted_iota(jnp.int32, (HD, W), 1) < HD
    return jnp.where(first, x[:HD], x[HD:])


def total_rows(total):
    high = total.astype(BF16).astype(F32)
    rest = total - high
    mid = rest.astype(BF16).astype(F32)
    low = rest - mid
    row = lax.broadcasted_iota(jnp.int32, (MSG - HD, W), 0)
    rows = jnp.where(row == 0, high, jnp.where(row == 1, mid, jnp.where(row == 2, low, 0.0)))
    return rows.astype(BF16)


def read_total(rows):
    return jnp.sum(rows.astype(F32), axis=0, keepdims=True)


def kernel(
    n_ctx,
    n,
    lq_ref,
    lk_ref,
    lv_ref,
    sq_ref,
    sk_ref,
    up_ref,
    dec_ref,
    mask_ref,
    gq_ref,
    gk_ref,
    gv_ref,
    k_buf,
    q_buf,
    u_buf,
    lg_buf,
    lg_out,
    bs_buf,
    bs_out,
    st_buf,
    st_out,
    re_buf,
    re_out,
    ri_buf,
    ri_out,
    c1_buf,
    c1_out,
    c2_buf,
    c2_out,
    weights,
    mixed,
    entries,
    leaving,
    scores,
    probs,
    loc_a,
    loc_b,
    acc_q,
    acc_k,
    acc_v,
    send_in,
    recv_in,
    send_mat,
    recv_mat,
    send_ctx,
    recv_ctx,
):
    here = lax.axis_index("ctx")
    me = lax.axis_index("head")
    chunks = n // 2
    scale = 1.0 / (HD * math.sqrt(HD))
    root_log2 = math.log2(math.e) / math.sqrt(HD)

    def peer_at(i):
        half = (i + 1) // 2
        odd = i % 2
        off = odd * half + (1 - odd) * (n - half)
        return (me + off) % n

    def lanes(p):
        return pl.ds(pl.multiple_of(p * W, W), W)

    def rounds(low, high, step, *carry):
        if carry:
            return lax.fori_loop(low, high, step, *carry)

        def plain(i, nothing):
            step(i)
            return nothing

        lax.fori_loop(low, high, plain, 0)

    barrier = pltpu.get_barrier_semaphore()

    def greet_head(i):
        pl.semaphore_signal(
            barrier, inc=1, device_id=(here, (me + i) % n), device_id_type=MESH
        )

    def greet_ctx(i):
        pl.semaphore_signal(
            barrier, inc=1, device_id=((here + i) % n_ctx, me), device_id_type=MESH
        )

    rounds(1, n, greet_head)
    rounds(1, n_ctx, greet_ctx)
    pl.semaphore_wait(barrier, n - 1 + n_ctx - 1)

    def in_copy(which, src, buf, peer, slot):
        return pltpu.make_async_remote_copy(
            src_ref=src.at[:, lanes(peer)],
            dst_ref=buf.at[slot],
            send_sem=send_in.at[which, peer],
            recv_sem=recv_in.at[which, slot],
            device_id=(here, peer),
            device_id_type=MESH,
        )

    def mat_copy(which, src, buf, peer, slot):
        return pltpu.make_async_remote_copy(
            src_ref=src.at[peer],
            dst_ref=buf.at[slot],
            send_sem=send_mat.at[which, peer],
            recv_sem=recv_mat.at[which, slot],
            device_id=(here, peer),
            device_id_type=MESH,
        )

    def ctx_copy(which, src, buf, peer, slot):
        return pltpu.make_async_remote_copy(
            src_ref=src,
            dst_ref=buf.at[slot],
            send_sem=send_ctx.at[which, peer],
            recv_sem=recv_ctx.at[which, slot],
            device_id=(peer, me),
            device_id_type=MESH,
        )

    inputs = ((sk_ref, k_buf), (sq_ref, q_buf), (up_ref, u_buf))
    for which, (src, buf) in enumerate(inputs):
        rounds(1, n, lambda i: in_copy(which, src, buf, peer_at(i), me).start())
        buf[me] = src[:, lanes(me)]

    tri = jnp.where(
        lax.broadcasted_iota(jnp.int32, (T, T), 1) <= lax.broadcasted_iota(jnp.int32, (T, T), 0),
        1.0,
        0.0,
    ).astype(BF16)

    def prepare(i):
        p = peer_at(i)
        heads = dec_ref.shape[1]
        columns, rows = [], []
        for h in range(2):
            pick = jnp.where(
                lax.broadcasted_iota(jnp.int32, (heads, T), 0) == 2 * p + h, 1.0, 0.0
            ).astype(BF16)
            spread_out = dot(dec_ref[...], pick).astype(BF16)
            columns.append(dot(tri, spread_out))
            rows.append(dot(spread_out, tri, 0, 1))
        lower = lax.broadcasted_iota(jnp.int32, (T, T), 1) <= lax.broadcasted_iota(
            jnp.int32, (T, T), 0
        )
        table = jnp.concatenate(
            [
                jnp.where(lower, jnp.exp(jnp.minimum(rows[h] - columns[h], 0.0)), 0.0)
                for h in range(2)
            ],
            axis=0,
        )
        weights[p] = table
        first = lax.broadcasted_iota(jnp.int32, (T, W), 1) < HD
        level = jnp.where(first, columns[0], columns[1])
        last = level[T - 1 : T]
        entries[p] = jnp.exp(-level)
        leave = jnp.exp(level - last)
        leaving[p] = leave
        lk = lk_ref[:, lanes(p)]
        lv = lv_ref[:, lanes(p)]
        sums = fold(dot_split(lk.astype(F32) * leave, lv, 0, 0))
        bs_out[p, :HD] = sums.astype(BF16)
        bs_out[p, HD:] = total_rows(jnp.exp(-last))

        @pl.when(i > 0)
        def _():
            mat_copy(0, bs_out, bs_buf, p, me).start()

        pair = dot(halves(lq_ref[:, lanes(p)]), lk, 1, 1)
        mixed[p] = (pair * table).astype(BF16)

    rounds(0, n, prepare)
    bs_buf[me] = bs_out[me]

    for which in range(2):
        src, buf = inputs[which]
        rounds(1, n, lambda i: in_copy(which, src, buf, peer_at(i), peer_at(i)).wait_recv())

    def soften(t):
        both = halves(q_buf[t])
        size = 2 * T

        def block_bias(c):
            upper = (mask_ref[t, 2 * c].astype(F32) - 1.0) * (-LOW)
            lower = (mask_ref[t, 2 * c + 1].astype(F32) - 1.0) * (-LOW)
            row = lax.broadcasted_iota(jnp.int32, (size, size), 0)
            return jnp.where(row < T, upper, lower)

        def score(c):
            keys = jnp.concatenate([k_buf[2 * c], k_buf[2 * c + 1]], axis=0)
            return dot(keys, both, 1, 1) + block_bias(c)

        def peak(x):
            return jnp.max(x.reshape(size // 8, 8, size), axis=0)

        def first_pass(c, highest):
            x = score(c)
            scores[c] = x
            return jnp.maximum(highest, peak(x))

        last = t // 2
        highest = rounds(0, last, first_pass, jnp.full((8, size), LOW, F32))
        key = last * size + lax.broadcasted_iota(jnp.int32, (size, size), 0)
        query = t * T + lax.broadcasted_iota(jnp.int32, (size, size), 1) % T
        x = jnp.where(key <= query, score(last), LOW)
        scores[last] = x
        highest = jnp.maximum(highest, peak(x))
        highest = jnp.max(highest, axis=0, keepdims=True)

        def second_pass(c, total):
            e = jnp.exp2((scores[c] - highest) * root_log2)
            scores[c] = e
            return total + jnp.sum(e.reshape(size // 8, 8, size), axis=0)

        total = rounds(0, last + 1, second_pass, jnp.zeros((8, size), F32))
        inverse = 1.0 / jnp.sum(total, axis=0, keepdims=True)

        def third_pass(c):
            probs[c, t] = (scores[c] * inverse).astype(BF16)

        rounds(0, last + 1, third_pass)

    rounds(0, n, soften)

    rounds(1, n, lambda i: in_copy(2, up_ref, u_buf, peer_at(i), peer_at(i)).wait_recv())

    my_chunk = me // 2

    def light(i):
        half = (i + 1) // 2
        odd = i % 2
        off = odd * half + (1 - odd) * (chunks - half)
        c = (my_chunk + off) % chunks

        def add(t, acc):
            return acc + dot(probs[c, t], halves(u_buf[t]))

        grad = rounds(2 * c, n, add, jnp.zeros((2 * T, W), F32)).astype(BF16)
        lg_out[2 * c] = grad[:T]
        lg_out[2 * c + 1] = grad[T:]
        for side in range(2):

            @pl.when(2 * c + side != me)
            def _():
                mat_copy(1, lg_out, lg_buf, 2 * c + side, me).start()

    rounds(0, chunks, light)
    lg_buf[me] = lg_out[me]

    zero_b = jnp.zeros((HD, W), F32)
    one_a = jnp.ones((1, W), F32)
    rounds(1, n, lambda i: mat_copy(0, bs_out, bs_buf, peer_at(i), peer_at(i)).wait_recv())

    def forward(b, carried):
        a, s = carried
        loc_a[0, b] = jnp.broadcast_to(a, (8, W))
        loc_b[0, b] = s
        total = read_total(bs_buf[b, HD:])
        return a * total, total * s + bs_buf[b, :HD].astype(F32)

    a, s = rounds(0, n, forward, (one_a, zero_b))
    c1_out[:HD] = s.astype(BF16)
    c1_out[HD:] = total_rows(a)
    rounds(here + 1, n_ctx, lambda k: ctx_copy(0, c1_out, c1_buf, k, here).start())

    def reach(i):
        p = peer_at(i)

        @pl.when(i > 0)
        def _():
            mat_copy(1, lg_out, lg_buf, p, p).wait_recv()

        moved = lq_ref[:, lanes(p)].astype(F32) * entries[p]
        re_out[p] = fold(dot_split(moved, lg_buf[p], 0, 0)).astype(BF16)

        @pl.when(i > 0)
        def _():
            mat_copy(2, re_out, re_buf, p, me).start()

    rounds(0, n, reach)
    re_buf[me] = re_out[me]

    def gather_forward(k, s):
        ctx_copy(0, c1_out, c1_buf, k, k).wait_recv()
        return read_total(c1_buf[k, HD:]) * s + c1_buf[k, :HD].astype(F32)

    span_in = rounds(0, here, gather_forward, zero_b)

    def send_state(i):
        b = peer_at(i)
        st_out[b] = (loc_a[0, b, :1] * span_in + loc_b[0, b]).astype(BF16)

        @pl.when(i > 0)
        def _():
            mat_copy(3, st_out, st_buf, b, me).start()

    rounds(0, n, send_state)
    st_buf[me] = st_out[me]

    rounds(1, n, lambda i: mat_copy(2, re_out, re_buf, peer_at(i), peer_at(i)).wait_recv())

    def backward(j, carried):
        b = n - 1 - j
        a, s = carried
        loc_a[1, b] = jnp.broadcast_to(a, (8, W))
        loc_b[1, b] = s
        total = read_total(bs_buf[b, HD:])
        return a * total, total * s + re_buf[b].astype(F32)

    a, s = rounds(0, n, backward, (one_a, zero_b))
    c2_out[:HD] = s.astype(BF16)
    c2_out[HD:] = total_rows(a)
    rounds(0, here, lambda k: ctx_copy(1, c2_out, c2_buf, k, here).start())

    def inside(p):
        lg2 = halves(lg_buf[p])
        lk = lk_ref[:, lanes(p)]
        lq = lq_ref[:, lanes(p)]
        back = (dot(lg2, lv_ref[:, lanes(p)], 1, 1) * weights[p]).astype(BF16)
        wide = jnp.concatenate([back[:T], back[T:]], axis=1)
        acc_q[p] = dot(wide, halves(lk))
        acc_k[p] = dot(back, halves(lq), 0, 0)
        acc_v[p] = dot(mixed[p], lg2, 0, 0)

    rounds(0, n, inside)

    def gather_backward(j, s):
        k = n_ctx - 1 - j
        ctx_copy(1, c2_out, c2_buf, k, k).wait_recv()
        return read_total(c2_buf[k, HD:]) * s + c2_buf[k, :HD].astype(F32)

    span_back = rounds(0, n_ctx - 1 - here, gather_backward, zero_b)

    def send_reach(i):
        b = peer_at(i)
        ri_out[b] = (loc_a[1, b, :1] * span_back + loc_b[1, b]).astype(BF16)

        @pl.when(i > 0)
        def _():
            mat_copy(4, ri_out, ri_buf, b, me).start()

    rounds(0, n, send_reach)
    ri_buf[me] = ri_out[me]

    def finish_query(i):
        p = peer_at(i)

        @pl.when(i > 0)
        def _():
            mat_copy(3, st_out, st_buf, p, p).wait_recv()

        carried = dot(lg_buf[p], halves(st_buf[p]), 1, 1)
        gq_ref[:, lanes(p)] = (scale * (acc_q[p] + entries[p] * carried)).astype(BF16)

    rounds(0, n, finish_query)

    def finish(i):
        p = peer_at(i)

        @pl.when(i > 0)
        def _():
            mat_copy(4, ri_out, ri_buf, p, p).wait_recv()

        both = halves(ri_buf[p])
        leave = leaving[p]
        from_value = dot(lv_ref[:, lanes(p)], both, 1, 1)
        from_key = dot(lk_ref[:, lanes(p)], both)
        gk_ref[:, lanes(p)] = (scale * (acc_k[p] + leave * from_value)).astype(BF16)
        gv_ref[:, lanes(p)] = (scale * (acc_v[p] + leave * from_key)).astype(BF16)

    rounds(0, n, finish)

    def drain(i):
        p = peer_at(i)
        for which, (src, buf) in enumerate(inputs):
            in_copy(which, src, buf, p, me).wait_send()
        mats = ((bs_out, bs_buf), (lg_out, lg_buf), (re_out, re_buf), (st_out, st_buf), (ri_out, ri_buf))
        for which, (src, buf) in enumerate(mats):
            mat_copy(which, src, buf, p, me).wait_send()

    rounds(1, n, drain)
    rounds(here + 1, n_ctx, lambda k: ctx_copy(0, c1_out, c1_buf, k, here).wait_send())
    rounds(0, here, lambda k: ctx_copy(1, c2_out, c2_buf, k, here).wait_send())


def body(n_ctx, n, *args):
    shape = args[0].shape
    vmem = pl.BlockSpec(memory_space=pltpu.VMEM)
    chunks = n // 2
    pairs = (n, T, W)
    mats = (n, HD, W)
    scratch = [
        pltpu.VMEM(pairs, BF16),
        pltpu.VMEM(pairs, BF16),
        pltpu.VMEM(pairs, BF16),
        pltpu.VMEM(pairs, BF16),
        pltpu.VMEM(pairs, BF16),
        pltpu.VMEM((n, MSG, W), BF16),
        pltpu.VMEM((n, MSG, W), BF16),
        pltpu.VMEM(mats, BF16),
        pltpu.VMEM(mats, BF16),
        pltpu.VMEM(mats, BF16),
        pltpu.VMEM(mats, BF16),
        pltpu.VMEM(mats, BF16),
        pltpu.VMEM(mats, BF16),
        pltpu.VMEM((n_ctx, MSG, W), BF16),
        pltpu.VMEM((MSG, W), BF16),
        pltpu.VMEM((n_ctx, MSG, W), BF16),
        pltpu.VMEM((MSG, W), BF16),
        pltpu.VMEM((n, 2 * T, T), F32),
        pltpu.VMEM((n, 2 * T, T), BF16),
        pltpu.VMEM(pairs, F32),
        pltpu.VMEM(pairs, F32),
        pltpu.VMEM((chunks, 2 * T, 2 * T), F32),
        pltpu.VMEM((chunks, n, 2 * T, 2 * T), BF16),
        pltpu.VMEM((2, n, 8, W), F32),
        pltpu.VMEM((2, n, HD, W), F32),
        pltpu.VMEM(pairs, F32),
        pltpu.VMEM(pairs, F32),
        pltpu.VMEM(pairs, F32),
        pltpu.SemaphoreType.DMA((3, n)),
        pltpu.SemaphoreType.DMA((3, n)),
        pltpu.SemaphoreType.DMA((5, n)),
        pltpu.SemaphoreType.DMA((5, n)),
        pltpu.SemaphoreType.DMA((2, n_ctx)),
        pltpu.SemaphoreType.DMA((2, n_ctx)),
    ]
    return pl.pallas_call(
        functools.partial(kernel, n_ctx, n),
        out_shape=[jax.ShapeDtypeStruct(shape, BF16)] * 3,
        in_specs=[vmem] * 7 + [pl.BlockSpec(memory_space=pltpu.SMEM)],
        out_specs=[vmem] * 3,
        scratch_shapes=scratch,
        compiler_params=pltpu.CompilerParams(
            collective_id=0, has_side_effects=True, vmem_limit_bytes=56 * 1024 * 1024
        ),
        name="span_backward",
    )(*args)


def solution(mesh):
    tokens = P(("ctx", "head"), None)
    return jax.shard_map(
        functools.partial(body, mesh.shape["ctx"], mesh.shape["head"]),
        mesh=mesh,
        in_specs=(tokens,) * 7 + (P("ctx", None),),
        out_specs=(tokens,) * 3,
        check_vma=False,
    )
```

```python
import functools
import math

import jax
import jax.numpy as jnp
from jax import lax
from jax.experimental import pallas as pl
from jax.experimental.pallas import tpu as pltpu
from jax.sharding import PartitionSpec as P

T = 128
W = 128
HD = 64
MSG = 80
LOW = -1e30
F32 = jnp.float32
BF16 = jnp.bfloat16
MESH = pl.DeviceIdType.MESH


def dot(a, b, ca=1, cb=0):
    return lax.dot_general(a, b, (((ca,), (cb,)), ((), ())), preferred_element_type=F32)


def dot_split(a, b, ca=1, cb=0):
    high = a.astype(BF16)
    low = (a - high.astype(F32)).astype(BF16)
    return dot(high, b, ca, cb) + dot(low, b, ca, cb)


def halves(x):
    first = lax.broadcasted_iota(jnp.int32, x.shape, 1) < HD
    zero = jnp.zeros_like(x)
    return jnp.concatenate([jnp.where(first, x, zero), jnp.where(first, zero, x)], axis=0)


def fold(x):
    first = lax.broadcasted_iota(jnp.int32, (HD, W), 1) < HD
    return jnp.where(first, x[:HD], x[HD:])


def total_rows(total):
    high = total.astype(BF16).astype(F32)
    rest = total - high
    mid = rest.astype(BF16).astype(F32)
    low = rest - mid
    row = lax.broadcasted_iota(jnp.int32, (MSG - HD, W), 0)
    rows = jnp.where(row == 0, high, jnp.where(row == 1, mid, jnp.where(row == 2, low, 0.0)))
    return rows.astype(BF16)


def read_total(rows):
    return jnp.sum(rows.astype(F32), axis=0, keepdims=True)


def kernel(
    n_ctx,
    n_y,
    n,
    lq_ref,
    lk_ref,
    lv_ref,
    sq_ref,
    sk_ref,
    up_ref,
    dec_ref,
    mask_ref,
    gq_ref,
    gk_ref,
    gv_ref,
    k_buf,
    q_buf,
    u_buf,
    lg_buf,
    lg_out,
    bs_buf,
    bs_out,
    st_buf,
    st_out,
    mv_buf,
    mv_out,
    ri_buf,
    ri_out,
    row_buf,
    row_out,
    col_buf,
    col_out,
    weights,
    level_rows,
    level_columns,
    reaches,
    u_wide,
    mixed,
    entries,
    leaving,
    scores,
    probs,
    loc_a,
    loc_b,
    acc_q,
    acc_k,
    acc_v,
    send_in,
    recv_in,
    send_mat,
    recv_mat,
    send_row,
    recv_row,
    send_col,
    recv_col,
):
    here = lax.axis_index("ctx")
    me = lax.axis_index("head")
    n_x = n_ctx // n_y
    x, y = here // n_y, here % n_y
    chunks = n // 2
    scale = 1.0 / (HD * math.sqrt(HD))
    root_log2 = math.log2(math.e) / math.sqrt(HD)

    def peer_at(i):
        half = (i + 1) // 2
        odd = i % 2
        off = odd * half + (1 - odd) * (n - half)
        return (me + off) % n

    def lanes(p):
        return pl.ds(pl.multiple_of(p * W, W), W)

    def rounds(low, high, step, *carry):
        if carry:
            return lax.fori_loop(low, high, step, *carry)

        def plain(i, nothing):
            step(i)
            return nothing

        lax.fori_loop(low, high, plain, 0)

    barrier = pltpu.get_barrier_semaphore()

    def greet_head(i):
        pl.semaphore_signal(
            barrier, inc=1, device_id=(here, (me + i) % n), device_id_type=MESH
        )

    def greet_ctx(k):
        pl.semaphore_signal(barrier, inc=1, device_id=(k, me), device_id_type=MESH)

    rounds(1, n, greet_head)
    rounds(1, n_y, lambda i: greet_ctx(x * n_y + (y + i) % n_y))
    rounds(1, n_x, lambda i: greet_ctx((x + i) % n_x * n_y + y))
    pl.semaphore_wait(barrier, n - 1 + n_y - 1 + n_x - 1)

    def in_copy(which, src, buf, peer, slot):
        return pltpu.make_async_remote_copy(
            src_ref=src.at[:, lanes(peer)],
            dst_ref=buf.at[slot],
            send_sem=send_in.at[which, peer],
            recv_sem=recv_in.at[which, slot],
            device_id=(here, peer),
            device_id_type=MESH,
        )

    def mat_copy(which, src, buf, peer, slot):
        return pltpu.make_async_remote_copy(
            src_ref=src.at[peer],
            dst_ref=buf.at[slot],
            send_sem=send_mat.at[which, peer],
            recv_sem=recv_mat.at[which, slot],
            device_id=(here, peer),
            device_id_type=MESH,
        )

    def row_copy(which, peer, slot):
        return pltpu.make_async_remote_copy(
            src_ref=row_out.at[which],
            dst_ref=row_buf.at[which, slot],
            send_sem=send_row.at[which, peer],
            recv_sem=recv_row.at[which, slot],
            device_id=(x * n_y + peer, me),
            device_id_type=MESH,
        )

    def col_copy(which, peer, slot):
        return pltpu.make_async_remote_copy(
            src_ref=col_out.at[which],
            dst_ref=col_buf.at[which, slot],
            send_sem=send_col.at[which, peer],
            recv_sem=recv_col.at[which, slot],
            device_id=(peer * n_y + y, me),
            device_id_type=MESH,
        )

    def pack(ref, a, s):
        ref[:HD] = s.astype(BF16)
        ref[HD:] = total_rows(a)

    def absorb(ref, carried):
        a, s = carried
        total = read_total(ref[HD:])
        return a * total, total * s + ref[:HD].astype(F32)

    def start_rows(which, a, s):
        pack(row_out.at[which], a, s)
        row_buf[which, y] = row_out[which]
        rounds(1, n_y, lambda i: row_copy(which, (y + i) % n_y, y).start())

    def fold_rows(which):
        def arrive(i):
            k = (y + i) % n_y
            row_copy(which, k, k).wait_recv()

        rounds(1, n_y, arrive)

        def step(i, carried):
            return absorb(row_buf.at[which, n_y - 1 - i if which else i], carried)

        mine = n_y - 1 - y if which else y
        part = rounds(0, mine, step, (one_a, zero_b))
        whole = rounds(mine, n_y, step, part)
        pack(col_out.at[which], *whole)
        low, high = (0, x) if which else (x + 1, n_x)
        rounds(low, high, lambda k: col_copy(which, k, x).start())
        return part

    def fold_columns(which, part):
        def step(i, carried):
            k = n_x - 1 - i if which else i
            col_copy(which, k, k).wait_recv()
            return absorb(col_buf.at[which, k], carried)

        other = rounds(0, n_x - 1 - x if which else x, step, (one_a, zero_b))
        return part[0] * other[1] + part[1]

    zero_b = jnp.zeros((HD, W), F32)
    one_a = jnp.ones((1, W), F32)
    inputs = ((sk_ref, k_buf), (sq_ref, q_buf), (up_ref, u_buf))
    for which, (src, buf) in enumerate(inputs):
        rounds(1, n, lambda i: in_copy(which, src, buf, peer_at(i), me).start())
        buf[me] = src[:, lanes(me)]

    lower = lax.broadcasted_iota(jnp.int32, (T, T), 1) <= lax.broadcasted_iota(
        jnp.int32, (T, T), 0
    )
    tri = jnp.where(lower, 1.0, 0.0).astype(BF16)
    heads = dec_ref.shape[0]
    level_rows[...] = dot(dec_ref[...], tri, 1, 1)

    def level_up(p):
        pick = jnp.where(
            lax.broadcasted_iota(jnp.int32, (heads, 2 * T), 0)
            == 2 * p + lax.broadcasted_iota(jnp.int32, (heads, 2 * T), 1) // T,
            1.0,
            0.0,
        ).astype(BF16)
        level_columns[p] = dot(tri, dot(dec_ref[...], pick, 0, 0).astype(BF16))

    for p in range(n):
        level_up(p)

    def prepare(i):
        p = peer_at(i)
        columns = [level_columns[p, :, h * T : (h + 1) * T] for h in range(2)]
        table = jnp.concatenate(
            [
                jnp.where(
                    lower,
                    jnp.exp(jnp.minimum(level_rows[pl.ds(2 * p + h, 1)] - columns[h], 0.0)),
                    0.0,
                )
                for h in range(2)
            ],
            axis=0,
        )
        weights[p] = table
        first = lax.broadcasted_iota(jnp.int32, (T, W), 1) < HD
        level = jnp.where(first, columns[0], columns[1])
        last = level[T - 1 : T]
        enter = jnp.exp(-level)
        entries[p] = enter
        leave = jnp.exp(level - last)
        leaving[p] = leave
        lk = lk_ref[:, lanes(p)]
        lv = lv_ref[:, lanes(p)]
        lq = lq_ref[:, lanes(p)]
        sums = fold(dot_split(lk.astype(F32) * leave, lv, 0, 0))
        bs_out[p, :HD] = sums.astype(BF16)
        bs_out[p, HD:] = total_rows(jnp.exp(-last))

        mv_out[p] = (lq.astype(F32) * enter).T.astype(BF16)

        @pl.when(i > 0)
        def _():
            mat_copy(2, mv_out, mv_buf, p, me).start()

        mixed[p] = (dot(halves(lq), lk, 1, 1) * table).astype(BF16)

    rounds(0, n, prepare)
    mv_buf[me] = mv_out[me]
    bs_buf[me] = bs_out[me]
    rounds(1, n, lambda i: mat_copy(0, bs_out, bs_buf, peer_at(i), me).start())

    for which in range(2):
        src, buf = inputs[which]
        rounds(1, n, lambda i: in_copy(which, src, buf, peer_at(i), peer_at(i)).wait_recv())

    def soften(u):
        size = 2 * T
        wide = 2 * size
        both = jnp.concatenate([halves(q_buf[2 * u]), halves(q_buf[2 * u + 1])], axis=0)

        def bias(c, a, b):
            return (mask_ref[2 * u + b, 2 * c + a].astype(F32) - 1.0) * (-LOW)

        def peak(x):
            return jnp.max(x.reshape(T // 8, 8, size), axis=0)

        def score(c):
            keys = k_buf[pl.ds(2 * c, 2)].reshape(size, W)
            return dot(keys, both, 1, 1)

        def part(x, a, b):
            return x[a * T : (a + 1) * T, b * size : (b + 1) * size]

        def keep(c, parts):
            for a in range(2):
                for b in range(2):
                    scores[c, a * T : (a + 1) * T, b * size : (b + 1) * size] = parts[a][b]
            return jnp.concatenate(
                [jnp.maximum(peak(parts[0][b]), peak(parts[1][b])) for b in range(2)], axis=1
            )

        def first_pass(c, highest):
            x = score(c)
            parts = [[part(x, a, b) + bias(c, a, b) for b in range(2)] for a in range(2)]
            return jnp.maximum(highest, keep(c, parts))

        highest = rounds(0, u, first_pass, jnp.full((8, wide), LOW, F32))
        key = lax.broadcasted_iota(jnp.int32, (T, size), 0)
        query = lax.broadcasted_iota(jnp.int32, (T, size), 1) % T
        x = score(u)
        parts = [
            [
                jnp.where(key <= query, part(x, 0, 0) + bias(u, 0, 0), LOW),
                part(x, 0, 1) + bias(u, 0, 1),
            ],
            [
                jnp.full((T, size), LOW, F32),
                jnp.where(key <= query, part(x, 1, 1) + bias(u, 1, 1), LOW),
            ],
        ]
        highest = jnp.maximum(highest, keep(u, parts))
        highest = jnp.max(highest, axis=0, keepdims=True)

        def second_pass(c, total):
            e = jnp.exp2((scores[c] - highest) * root_log2)
            scores[c] = e
            return total + jnp.sum(e.reshape(size // 8, 8, wide), axis=0)

        total = rounds(0, u + 1, second_pass, jnp.zeros((8, wide), F32))
        inverse = 1.0 / jnp.sum(total, axis=0, keepdims=True)

        def third_pass(c):
            probs[c, u] = (scores[c] * inverse).astype(BF16)

        rounds(0, u + 1, third_pass)

    rounds(0, chunks, soften)

    rounds(1, n, lambda i: in_copy(2, up_ref, u_buf, peer_at(i), peer_at(i)).wait_recv())

    def widen(u):
        u_wide[u] = jnp.concatenate([halves(u_buf[2 * u]), halves(u_buf[2 * u + 1])], axis=0)

    rounds(0, chunks, widen)

    my_chunk = me // 2

    def light(i):
        half = (i + 1) // 2
        odd = i % 2
        off = odd * half + (1 - odd) * (chunks - half)
        c = (my_chunk + off) % chunks

        def add(u, acc):
            return acc + dot(probs[c, u], u_wide[u])

        grad = rounds(c, chunks, add, jnp.zeros((2 * T, W), F32)).astype(BF16)
        lg_out[2 * c] = grad[:T]
        lg_out[2 * c + 1] = grad[T:]
        for side in range(2):

            @pl.when(2 * c + side != me)
            def _():
                mat_copy(1, lg_out, lg_buf, 2 * c + side, me).start()

    rounds(0, chunks, light)
    lg_buf[me] = lg_out[me]

    rounds(1, n, lambda i: mat_copy(0, bs_out, bs_buf, peer_at(i), peer_at(i)).wait_recv())

    def forward(b, carried):
        a, s = carried
        loc_a[0, b] = jnp.broadcast_to(a, (8, W))
        loc_b[0, b] = s
        return absorb(bs_buf.at[b], carried)

    start_rows(0, *rounds(0, n, forward, (one_a, zero_b)))

    rounds(1, n, lambda i: mat_copy(2, mv_out, mv_buf, peer_at(i), peer_at(i)).wait_recv())

    def reach(b):
        reaches[b] = fold(dot(mv_buf[b], lg_out[b]))

    rounds(0, n, reach)

    def backward(j, carried):
        b = n - 1 - j
        a, s = carried
        loc_a[1, b] = jnp.broadcast_to(a, (8, W))
        loc_b[1, b] = s
        total = read_total(bs_buf[b, HD:])
        return a * total, total * s + reaches[b]

    start_rows(1, *rounds(0, n, backward, (one_a, zero_b)))
    part_in = fold_rows(0)
    part_back = fold_rows(1)

    span_in = fold_columns(0, part_in)

    def send_state(i):
        b = peer_at(i)
        st_out[b] = (loc_a[0, b, :1] * span_in + loc_b[0, b]).astype(BF16)

        @pl.when(i > 0)
        def _():
            mat_copy(3, st_out, st_buf, b, me).start()

    rounds(0, n, send_state)
    st_buf[me] = st_out[me]

    span_back = fold_columns(1, part_back)

    def send_reach(i):
        b = peer_at(i)
        ri_out[b] = (loc_a[1, b, :1] * span_back + loc_b[1, b]).astype(BF16)

        @pl.when(i > 0)
        def _():
            mat_copy(4, ri_out, ri_buf, b, me).start()

    rounds(0, n, send_reach)
    ri_buf[me] = ri_out[me]

    def inside(i):
        p = peer_at(i)

        @pl.when(i > 0)
        def _():
            mat_copy(1, lg_out, lg_buf, p, p).wait_recv()

        lg2 = halves(lg_buf[p])
        lk = lk_ref[:, lanes(p)]
        lq = lq_ref[:, lanes(p)]
        back = (dot(lg2, lv_ref[:, lanes(p)], 1, 1) * weights[p]).astype(BF16)
        wide = jnp.concatenate([back[:T], back[T:]], axis=1)
        acc_q[p] = dot(wide, halves(lk))
        acc_k[p] = dot(back, halves(lq), 0, 0)
        acc_v[p] = dot(mixed[p], lg2, 0, 0)

    rounds(0, n, inside)

    def finish_query(i):
        p = peer_at(i)

        @pl.when(i > 0)
        def _():
            mat_copy(3, st_out, st_buf, p, p).wait_recv()

        carried = dot(lg_buf[p], halves(st_buf[p]), 1, 1)
        gq_ref[:, lanes(p)] = (scale * (acc_q[p] + entries[p] * carried)).astype(BF16)

    rounds(0, n, finish_query)

    def finish(i):
        p = peer_at(i)

        @pl.when(i > 0)
        def _():
            mat_copy(4, ri_out, ri_buf, p, p).wait_recv()

        both = halves(ri_buf[p])
        leave = leaving[p]
        from_value = dot(lv_ref[:, lanes(p)], both, 1, 1)
        from_key = dot(lk_ref[:, lanes(p)], both)
        gk_ref[:, lanes(p)] = (scale * (acc_k[p] + leave * from_value)).astype(BF16)
        gv_ref[:, lanes(p)] = (scale * (acc_v[p] + leave * from_key)).astype(BF16)

    rounds(0, n, finish)

    def drain(i):
        p = peer_at(i)
        for which, (src, buf) in enumerate(inputs):
            in_copy(which, src, buf, p, me).wait_send()
        mats = ((bs_out, bs_buf), (lg_out, lg_buf), (mv_out, mv_buf), (st_out, st_buf), (ri_out, ri_buf))
        for which, (src, buf) in enumerate(mats):
            mat_copy(which, src, buf, p, me).wait_send()

    rounds(1, n, drain)
    for which in range(2):
        rounds(1, n_y, lambda i: row_copy(which, (y + i) % n_y, y).wait_send())
        low, high = (0, x) if which else (x + 1, n_x)
        rounds(low, high, lambda k: col_copy(which, k, x).wait_send())


def body(n_ctx, n, *args):
    shape = args[0].shape
    args = (*args[:6], args[6].T, args[7])
    vmem = pl.BlockSpec(memory_space=pltpu.VMEM)
    n_y = 8 if n_ctx % 8 == 0 else 2
    n_x = n_ctx // n_y
    chunks = n // 2
    pairs = (n, T, W)
    mats = (n, HD, W)
    scratch = [
        pltpu.VMEM(pairs, BF16),
        pltpu.VMEM(pairs, BF16),
        pltpu.VMEM(pairs, BF16),
        pltpu.VMEM(pairs, BF16),
        pltpu.VMEM(pairs, BF16),
        pltpu.VMEM((n, MSG, W), BF16),
        pltpu.VMEM((n, MSG, W), BF16),
        pltpu.VMEM(mats, BF16),
        pltpu.VMEM(mats, BF16),
        pltpu.VMEM(pairs, BF16),
        pltpu.VMEM(pairs, BF16),
        pltpu.VMEM(mats, BF16),
        pltpu.VMEM(mats, BF16),
        pltpu.VMEM((2, n_y, MSG, W), BF16),
        pltpu.VMEM((2, MSG, W), BF16),
        pltpu.VMEM((2, n_x, MSG, W), BF16),
        pltpu.VMEM((2, MSG, W), BF16),
        pltpu.VMEM((n, 2 * T, T), F32),
        pltpu.VMEM((2 * n, T), F32),
        pltpu.VMEM((n, T, 2 * T), F32),
        pltpu.VMEM(mats, F32),
        pltpu.VMEM((chunks, 4 * T, W), BF16),
        pltpu.VMEM((n, 2 * T, T), BF16),
        pltpu.VMEM(pairs, F32),
        pltpu.VMEM(pairs, F32),
        pltpu.VMEM((chunks, 2 * T, 4 * T), F32),
        pltpu.VMEM((chunks, chunks, 2 * T, 4 * T), BF16),
        pltpu.VMEM((2, n, 8, W), F32),
        pltpu.VMEM((2, n, HD, W), F32),
        pltpu.VMEM(pairs, F32),
        pltpu.VMEM(pairs, F32),
        pltpu.VMEM(pairs, F32),
        pltpu.SemaphoreType.DMA((3, n)),
        pltpu.SemaphoreType.DMA((3, n)),
        pltpu.SemaphoreType.DMA((5, n)),
        pltpu.SemaphoreType.DMA((5, n)),
        pltpu.SemaphoreType.DMA((2, n_y)),
        pltpu.SemaphoreType.DMA((2, n_y)),
        pltpu.SemaphoreType.DMA((2, n_x)),
        pltpu.SemaphoreType.DMA((2, n_x)),
    ]
    return pl.pallas_call(
        functools.partial(kernel, n_ctx, n_y, n),
        out_shape=[jax.ShapeDtypeStruct(shape, BF16)] * 3,
        in_specs=[vmem] * 7 + [pl.BlockSpec(memory_space=pltpu.SMEM)],
        out_specs=[vmem] * 3,
        scratch_shapes=scratch,
        compiler_params=pltpu.CompilerParams(
            collective_id=0, has_side_effects=True, vmem_limit_bytes=56 * 1024 * 1024
        ),
        name="span_backward",
    )(*args)


def solution(mesh):
    tokens = P(("ctx", "head"), None)
    return jax.shard_map(
        functools.partial(body, mesh.shape["ctx"], mesh.shape["head"]),
        mesh=mesh,
        in_specs=(tokens,) * 7 + (P("ctx", None),),
        out_specs=(tokens,) * 3,
        check_vma=False,
    )
```

```python
import functools
import math

import jax
import jax.numpy as jnp
from jax import lax
from jax.experimental import pallas as pl
from jax.experimental.pallas import tpu as pltpu
from jax.sharding import PartitionSpec as P

T = 128
W = 128
HD = 64
MSG = 80
LOW = -1e30
F32 = jnp.float32
BF16 = jnp.bfloat16
MESH = pl.DeviceIdType.MESH


def dot(a, b, ca=1, cb=0):
    return lax.dot_general(a, b, (((ca,), (cb,)), ((), ())), preferred_element_type=F32)


def dot_split(a, b, ca=1, cb=0):
    high = a.astype(BF16)
    low = (a - high.astype(F32)).astype(BF16)
    return dot(high, b, ca, cb) + dot(low, b, ca, cb)


def halves(x):
    first = lax.broadcasted_iota(jnp.int32, x.shape, 1) < HD
    zero = jnp.zeros_like(x)
    return jnp.concatenate([jnp.where(first, x, zero), jnp.where(first, zero, x)], axis=0)


def fold(x):
    first = lax.broadcasted_iota(jnp.int32, (HD, W), 1) < HD
    return jnp.where(first, x[:HD], x[HD:])


def total_rows(total):
    high = total.astype(BF16).astype(F32)
    rest = total - high
    mid = rest.astype(BF16).astype(F32)
    low = rest - mid
    row = lax.broadcasted_iota(jnp.int32, (MSG - HD, W), 0)
    rows = jnp.where(row == 0, high, jnp.where(row == 1, mid, jnp.where(row == 2, low, 0.0)))
    return rows.astype(BF16)


def two_totals(first, second):
    upper, lower = total_rows(first), total_rows(second)
    return jnp.concatenate([upper[:8].astype(F32), lower[:8].astype(F32)], axis=0).astype(BF16)


def read_two(rows):
    rows = rows.astype(F32)
    return (
        jnp.sum(rows[:8], axis=0, keepdims=True),
        jnp.sum(rows[8:], axis=0, keepdims=True),
    )


def read_total(rows):
    return jnp.sum(rows.astype(F32), axis=0, keepdims=True)


def kernel(
    n_ctx,
    n_y,
    n,
    lq_hbm,
    lk_hbm,
    lv_hbm,
    sq_ref,
    sk_ref,
    up_ref,
    dec_ref,
    mask_ref,
    gq_ref,
    gk_ref,
    gv_ref,
    lq_ref,
    lk_ref,
    lv_ref,
    k_buf,
    q_buf,
    u_buf,
    lg_buf,
    lg_out,
    bs_mate,
    bs_out,
    cs_buf,
    cs_out,
    st_buf,
    st_out,
    mv_buf,
    mv_out,
    ri_buf,
    ri_out,
    row_buf,
    row_out,
    col_buf,
    col_out,
    weights,
    weights_t,
    level_rows,
    level_columns,
    reaches,
    u_wide,
    mixed,
    entries,
    leaving,
    scores,
    probs,
    loc_a,
    loc_b,
    acc_q,
    acc_k,
    acc_v,
    send_in,
    recv_in,
    send_mat,
    recv_mat,
    send_row,
    recv_row,
    send_col,
    recv_col,
    send_chip,
    recv_chip,
    send_mate,
    recv_mate,
    local_sem,
):
    here = lax.axis_index("ctx")
    me = lax.axis_index("head")
    n_x = n_ctx // n_y
    x, y = here // n_y, here % n_y
    chunks = n // 2
    chips = n // 2
    chip, core = me // 2, me % 2
    mate = me + 1 - 2 * core
    root_log2 = math.log2(math.e) / math.sqrt(HD)

    def peer_at(i):
        half = (i + 1) // 2
        odd = i % 2
        off = odd * half + (1 - odd) * (n - half)
        return (me + off) % n

    def lanes(p):
        return pl.ds(pl.multiple_of(p * W, W), W)

    def rounds(low, high, step, *carry):
        if carry:
            return lax.fori_loop(low, high, step, *carry)

        def plain(i, nothing):
            step(i)
            return nothing

        lax.fori_loop(low, high, plain, 0)

    def several(count, step, low=0, high=n):
        def turn(j):
            for q in range(count):
                step(count * j + q)

        rounds(low // count, high // count, turn)

    barrier = pltpu.get_barrier_semaphore()

    def greet_head(i):
        pl.semaphore_signal(
            barrier, inc=1, device_id=(here, (me + i) % n), device_id_type=MESH
        )

    def greet_ctx(k):
        pl.semaphore_signal(barrier, inc=1, device_id=(k, me), device_id_type=MESH)

    rounds(1, n, greet_head)
    rounds(1, n_y, lambda i: greet_ctx(x * n_y + (y + i) % n_y))
    rounds(1, n_x, lambda i: greet_ctx((x + i) % n_x * n_y + y))
    light = ((lq_hbm, lq_ref), (lk_hbm, lk_ref), (lv_hbm, lv_ref))
    light_copies = [
        pltpu.make_async_copy(src, dst, local_sem.at[3 + which])
        for which, (src, dst) in enumerate(light)
    ]
    for copy in light_copies:
        copy.start()
    pl.semaphore_wait(barrier, n - 1 + n_y - 1 + n_x - 1)

    def in_copy(which, src, buf, peer, slot):
        return pltpu.make_async_remote_copy(
            src_ref=src.at[:, lanes(peer)],
            dst_ref=buf.at[slot],
            send_sem=send_in.at[which, peer],
            recv_sem=recv_in.at[which, slot],
            device_id=(here, peer),
            device_id_type=MESH,
        )

    def mat_copy(which, src, buf, peer, slot):
        return pltpu.make_async_remote_copy(
            src_ref=src.at[peer],
            dst_ref=buf.at[slot],
            send_sem=send_mat.at[which, peer],
            recv_sem=recv_mat.at[which, slot],
            device_id=(here, peer),
            device_id_type=MESH,
        )

    def chip_copy(which, src, dst, peer, slot):
        return pltpu.make_async_remote_copy(
            src_ref=src,
            dst_ref=dst,
            send_sem=send_chip.at[which, peer],
            recv_sem=recv_chip.at[which, slot],
            device_id=(here, 2 * peer + core),
            device_id_type=MESH,
        )

    def sum_copy(peer, slot):
        return chip_copy(0, cs_out.at[peer], cs_buf.at[slot], peer, slot)

    def state_copy(peer, slot):
        return chip_copy(1, st_out.at[peer], st_buf.at[core, slot], peer, slot)

    def mate_copy(which, src, dst):
        return pltpu.make_async_remote_copy(
            src_ref=src,
            dst_ref=dst,
            send_sem=send_mate.at[which],
            recv_sem=recv_mate.at[which],
            device_id=(here, mate),
            device_id_type=MESH,
        )

    def chip_at(i):
        half = (i + 1) // 2
        odd = i % 2
        return (chip + odd * half + (1 - odd) * (chips - half)) % chips

    def row_copy(which, peer, slot):
        return pltpu.make_async_remote_copy(
            src_ref=row_out.at[which],
            dst_ref=row_buf.at[which, slot],
            send_sem=send_row.at[which, peer],
            recv_sem=recv_row.at[which, slot],
            device_id=(x * n_y + peer, me),
            device_id_type=MESH,
        )

    def col_copy(which, peer, slot):
        return pltpu.make_async_remote_copy(
            src_ref=col_out.at[which],
            dst_ref=col_buf.at[which, slot],
            send_sem=send_col.at[which, peer],
            recv_sem=recv_col.at[which, slot],
            device_id=(peer * n_y + y, me),
            device_id_type=MESH,
        )

    def pack(ref, a, s):
        ref[:HD] = s.astype(BF16)
        ref[HD:] = total_rows(a)

    def absorb(ref, carried):
        a, s = carried
        total = read_total(ref[HD:])
        return a * total, total * s + ref[:HD].astype(F32)

    def start_rows(which, a, s):
        pack(row_out.at[which], a, s)
        row_buf[which, y] = row_out[which]
        rounds(1, n_y, lambda i: row_copy(which, (y + i) % n_y, y).start())

    def fold_rows(which):
        def arrive(i):
            k = (y + i) % n_y
            row_copy(which, k, k).wait_recv()

        rounds(1, n_y, arrive)

        def step(i, carried):
            return absorb(row_buf.at[which, n_y - 1 - i if which else i], carried)

        mine = n_y - 1 - y if which else y
        part = rounds(0, mine, step, (one_a, zero_b))
        whole = rounds(mine, n_y, step, part)
        pack(col_out.at[which], *whole)
        low, high = (0, x) if which else (x + 1, n_x)
        rounds(low, high, lambda k: col_copy(which, k, x).start())
        return part

    def fold_columns(which, part):
        def step(i, carried):
            k = n_x - 1 - i if which else i
            col_copy(which, k, k).wait_recv()
            return absorb(col_buf.at[which, k], carried)

        other = rounds(0, n_x - 1 - x if which else x, step, (one_a, zero_b))
        return part[0] * other[1] + part[1]

    zero_b = jnp.zeros((HD, W), F32)
    one_a = jnp.ones((1, W), F32)
    inputs = ((sk_ref, k_buf), (sq_ref, q_buf), (up_ref, u_buf))
    for which, (src, buf) in enumerate(inputs):
        rounds(1, n, lambda i: in_copy(which, src, buf, peer_at(i), me).start())

    own_copies = [
        pltpu.make_async_copy(src.at[:, lanes(me)], buf.at[me], local_sem.at[which])
        for which, (src, buf) in enumerate(inputs)
    ]
    for copy in own_copies:
        copy.start()

    lower = lax.broadcasted_iota(jnp.int32, (T, T), 1) <= lax.broadcasted_iota(
        jnp.int32, (T, T), 0
    )
    tri = jnp.where(lower, 1.0, 0.0).astype(BF16)
    heads = dec_ref.shape[0]
    level_rows[...] = dot(dec_ref[...], tri, 1, 1)

    def level_up(p):
        pick = jnp.where(
            lax.broadcasted_iota(jnp.int32, (heads, 2 * T), 0)
            == 2 * p + lax.broadcasted_iota(jnp.int32, (heads, 2 * T), 1) // T,
            1.0,
            0.0,
        ).astype(BF16)
        level_columns[p] = dot(tri, dot(dec_ref[...], pick, 0, 0).astype(BF16))

    for p in range(n):
        level_up(p)

    for copy in light_copies:
        copy.wait()

    def prepare(i):
        p = peer_at(i)
        columns = [level_columns[p, :, h * T : (h + 1) * T] for h in range(2)]
        table = jnp.concatenate(
            [
                jnp.where(
                    lower,
                    jnp.exp(jnp.minimum(level_rows[pl.ds(2 * p + h, 1)] - columns[h], 0.0)),
                    0.0,
                )
                for h in range(2)
            ],
            axis=0,
        )
        table_t = jnp.concatenate([table[:T].T, table[T:].T], axis=1)
        weights[p] = table
        weights_t[p] = table_t
        first = lax.broadcasted_iota(jnp.int32, (T, W), 1) < HD
        level = jnp.where(first, columns[0], columns[1])
        last = level[T - 1 : T]
        enter = jnp.exp(-level)
        entries[p] = enter
        leave = jnp.exp(level - last)
        leaving[p] = leave
        lk = lk_ref[:, lanes(p)]
        lv = lv_ref[:, lanes(p)]
        lq = lq_ref[:, lanes(p)]
        sums = fold(dot_split(lk.astype(F32) * leave, lv, 0, 0))
        bs_out[p, :HD] = sums.astype(BF16)
        bs_out[p, HD:] = total_rows(jnp.exp(-last))

        mv_out[p] = (lq.astype(F32) * enter).T.astype(BF16)

        @pl.when(i > 0)
        def _():
            mat_copy(2, mv_out, mv_buf, p, me).start()

        mixed[p] = (dot(lk, halves(lq), 1, 1) * table_t).astype(BF16)

    rounds(0, n, prepare)
    mv_buf[me] = mv_out[me]
    sums_to_mate = mate_copy(0, bs_out, bs_mate)
    sums_to_mate.start()

    for which in range(2):
        src, buf = inputs[which]
        rounds(1, n, lambda i: in_copy(which, src, buf, peer_at(i), peer_at(i)).wait_recv())
        own_copies[which].wait()

    def soften(u):
        size = 2 * T
        wide = 2 * size
        both = jnp.concatenate([halves(q_buf[2 * u]), halves(q_buf[2 * u + 1])], axis=0)

        def bias(c, a, b):
            return (mask_ref[2 * u + b, 2 * c + a].astype(F32) - 1.0) * (-LOW)

        def peak(x):
            return jnp.max(x.reshape(T // 8, 8, size), axis=0)

        def score(c):
            keys = k_buf[pl.ds(2 * c, 2)].reshape(size, W)
            return dot(keys, both, 1, 1)

        def part(x, a, b):
            return x[a * T : (a + 1) * T, b * size : (b + 1) * size]

        def keep(c, parts):
            for a in range(2):
                for b in range(2):
                    scores[c, a * T : (a + 1) * T, b * size : (b + 1) * size] = parts[a][b]
            return jnp.concatenate(
                [jnp.maximum(peak(parts[0][b]), peak(parts[1][b])) for b in range(2)], axis=1
            )

        def first_pass(c, highest):
            x = score(c)
            parts = [[part(x, a, b) + bias(c, a, b) for b in range(2)] for a in range(2)]
            return jnp.maximum(highest, keep(c, parts))

        highest = rounds(0, u, first_pass, jnp.full((8, wide), LOW, F32))
        key = lax.broadcasted_iota(jnp.int32, (T, size), 0)
        query = lax.broadcasted_iota(jnp.int32, (T, size), 1) % T
        x = score(u)
        parts = [
            [
                jnp.where(key <= query, part(x, 0, 0) + bias(u, 0, 0), LOW),
                part(x, 0, 1) + bias(u, 0, 1),
            ],
            [
                jnp.full((T, size), LOW, F32),
                jnp.where(key <= query, part(x, 1, 1) + bias(u, 1, 1), LOW),
            ],
        ]
        highest = jnp.maximum(highest, keep(u, parts))
        highest = jnp.max(highest, axis=0, keepdims=True)

        def second_pass(c, total):
            e = jnp.exp2((scores[c] - highest) * root_log2)
            scores[c] = e
            return total + jnp.sum(e.reshape(size // 8, 8, wide), axis=0)

        total = rounds(0, u + 1, second_pass, jnp.zeros((8, wide), F32))
        inverse = 1.0 / jnp.sum(total, axis=0, keepdims=True)

        def third_pass(c):
            probs[c, u] = (scores[c] * inverse).astype(BF16)

        rounds(0, u + 1, third_pass)

    rounds(0, chunks, soften)

    sums_to_mate.wait_recv()

    def join(i):
        peer = chip_at(i)
        p = 2 * peer + core
        mine, other = bs_out[p, :HD].astype(F32), bs_mate[p, :HD].astype(F32)
        mine_a, other_a = read_total(bs_out[p, HD:]), read_total(bs_mate[p, HD:])
        early = jnp.where(core == 0, mine, other)
        late = jnp.where(core == 0, other, mine)
        early_a = jnp.where(core == 0, mine_a, other_a)
        late_a = jnp.where(core == 0, other_a, mine_a)
        cs_out[peer, :HD] = (late_a * early + late).astype(BF16)
        cs_out[peer, HD:] = two_totals(early_a, late_a)

        @pl.when(i > 0)
        def _():
            sum_copy(peer, chip).start()

    rounds(0, chips, join)
    cs_buf[chip] = cs_out[chip]

    rounds(1, n, lambda i: in_copy(2, up_ref, u_buf, peer_at(i), peer_at(i)).wait_recv())
    own_copies[2].wait()

    def widen(u):
        u_wide[u] = jnp.concatenate([halves(u_buf[2 * u]), halves(u_buf[2 * u + 1])], axis=0)

    rounds(0, chunks, widen)

    my_chunk = me // 2

    def light_pair(i):
        half = (i + 1) // 2
        odd = i % 2
        off = odd * half + (1 - odd) * (chunks - half)
        c = (my_chunk + off) % chunks

        def add(u, acc):
            return acc + dot(probs[c, u], u_wide[u])

        grad = rounds(c, chunks, add, jnp.zeros((2 * T, W), F32)).astype(BF16)
        lg_out[2 * c] = grad[:T]
        lg_out[2 * c + 1] = grad[T:]
        for side in range(2):

            @pl.when(2 * c + side != me)
            def _():
                mat_copy(1, lg_out, lg_buf, 2 * c + side, me).start()

    rounds(0, chunks, light_pair)
    lg_buf[me] = lg_out[me]

    rounds(1, n, lambda i: mat_copy(2, mv_out, mv_buf, peer_at(i), peer_at(i)).wait_recv())

    def reach(b):
        reaches[b] = fold(dot(mv_buf[b], lg_out[b]))

    several(4, reach)

    rounds(1, chips, lambda i: sum_copy(chip_at(i), chip_at(i)).wait_recv())

    def forward(c, carried):
        a, s = carried
        loc_a[0, c] = jnp.broadcast_to(a, (8, W))
        loc_b[0, c] = s
        early_a, late_a = read_two(cs_buf[c, HD:])
        total = early_a * late_a
        return a * total, total * s + cs_buf[c, :HD].astype(F32)

    start_rows(0, *rounds(0, chips, forward, (one_a, zero_b)))

    def backward(j, carried):
        c = chips - 1 - j
        totals = read_two(cs_buf[c, HD:])
        a, s = carried
        for side in (1, 0):
            loc_a[1, 2 * c + side] = jnp.broadcast_to(a, (8, W))
            loc_b[1, 2 * c + side] = s
            a, s = a * totals[side], totals[side] * s + reaches[2 * c + side]
        return a, s

    start_rows(1, *rounds(0, chips, backward, (one_a, zero_b)))

    span_in = fold_columns(0, fold_rows(0))

    def send_state(i):
        c = chip_at(i)
        st_out[c] = (loc_a[0, c, :1] * span_in + loc_b[0, c]).astype(BF16)

        @pl.when(i > 0)
        def _():
            state_copy(c, chip).start()

    rounds(0, chips, send_state)
    st_buf[core, chip] = st_out[chip]

    part_back = fold_rows(1)
    span_back = fold_columns(1, part_back)

    def send_reach(i):
        b = peer_at(i)
        ri_out[b] = (loc_a[1, b, :1] * span_back + loc_b[1, b]).astype(BF16)

        @pl.when(i > 0)
        def _():
            mat_copy(4, ri_out, ri_buf, b, me).start()

    rounds(0, n, send_reach)
    ri_buf[me] = ri_out[me]

    rounds(1, n, lambda i: mat_copy(1, lg_out, lg_buf, peer_at(i), peer_at(i)).wait_recv())

    def inside(p):
        lg2 = halves(lg_buf[p])
        lk = lk_ref[:, lanes(p)]
        lv = lv_ref[:, lanes(p)]
        lq = lq_ref[:, lanes(p)]
        back = (dot(lg2, lv, 1, 1) * weights[p]).astype(BF16)
        back_t = (dot(lv, lg2, 1, 1) * weights_t[p]).astype(BF16)
        wide = jnp.concatenate([back[:T], back[T:]], axis=1)
        acc_q[p] = dot(wide, halves(lk))
        acc_k[p] = dot(back_t, halves(lq))
        acc_v[p] = dot(mixed[p], lg2)

    several(2, inside, 0, n // 2)

    rounds(1, chips, lambda i: state_copy(chip_at(i), chip_at(i)).wait_recv())
    states_to_mate = mate_copy(1, st_buf.at[core], st_buf.at[core])
    states_to_mate.start()

    several(2, inside, n // 2, n)
    states_to_mate.wait_recv()

    def finish_query(p):
        state = st_buf[p % 2, p // 2].astype(F32)
        passed = read_total(bs_mate[p, HD:]) * state + bs_mate[p, :HD].astype(F32)
        state = jnp.where(core == 1, passed, state)
        high = state.astype(BF16)
        low = (state - high.astype(F32)).astype(BF16)
        lg = lg_buf[p]
        carried = dot(lg, halves(high), 1, 1) + dot(lg, halves(low), 1, 1)
        gq_ref[:, lanes(p)] = (acc_q[p] + entries[p] * carried).astype(BF16)

    several(2, finish_query)

    def finish(p):
        both = halves(ri_buf[p])
        leave = leaving[p]
        from_value = dot(lv_ref[:, lanes(p)], both, 1, 1)
        from_key = dot(lk_ref[:, lanes(p)], both)
        gk_ref[:, lanes(p)] = (acc_k[p] + leave * from_value).astype(BF16)
        gv_ref[:, lanes(p)] = (acc_v[p] + leave * from_key).astype(BF16)

    def finish_two(j):
        first, second = peer_at(2 * j), peer_at(2 * j + 1)

        @pl.when(j > 0)
        def _():
            mat_copy(4, ri_out, ri_buf, first, first).wait_recv()

        mat_copy(4, ri_out, ri_buf, second, second).wait_recv()
        finish(first)
        finish(second)

    rounds(0, n // 2, finish_two)

    def drain(i):
        p = peer_at(i)
        for which, (src, buf) in enumerate(inputs):
            in_copy(which, src, buf, p, me).wait_send()
        for which, src, buf in ((1, lg_out, lg_buf), (2, mv_out, mv_buf), (4, ri_out, ri_buf)):
            mat_copy(which, src, buf, p, me).wait_send()

    rounds(1, n, drain)

    def drain_chip(i):
        sum_copy(chip_at(i), chip).wait_send()
        state_copy(chip_at(i), chip).wait_send()

    rounds(1, chips, drain_chip)
    sums_to_mate.wait_send()
    states_to_mate.wait_send()
    for which in range(2):
        rounds(1, n_y, lambda i: row_copy(which, (y + i) % n_y, y).wait_send())
        low, high = (0, x) if which else (x + 1, n_x)
        rounds(low, high, lambda k: col_copy(which, k, x).wait_send())


def scale_kernel(*refs):
    scale = 1.0 / (HD * math.sqrt(HD))
    for src, dst in zip(refs[:3], refs[3:]):
        dst[...] = (src[...].astype(F32) * scale).astype(BF16)


def body(n_ctx, n, *args):
    shape = args[0].shape
    args = (*args[:6], args[6].T, args[7])
    vmem = pl.BlockSpec(memory_space=pltpu.VMEM)
    n_y = 8 if n_ctx % 8 == 0 else 2
    n_x = n_ctx // n_y
    chunks = n // 2
    pairs = (n, T, W)
    mats = (n, HD, W)
    scratch = [
        pltpu.VMEM(shape, BF16),
        pltpu.VMEM(shape, BF16),
        pltpu.VMEM(shape, BF16),
        pltpu.VMEM(pairs, BF16),
        pltpu.VMEM(pairs, BF16),
        pltpu.VMEM(pairs, BF16),
        pltpu.VMEM(pairs, BF16),
        pltpu.VMEM(pairs, BF16),
        pltpu.VMEM((n, MSG, W), BF16),
        pltpu.VMEM((n, MSG, W), BF16),
        pltpu.VMEM((chunks, MSG, W), BF16),
        pltpu.VMEM((chunks, MSG, W), BF16),
        pltpu.VMEM((2, chunks, HD, W), BF16),
        pltpu.VMEM((chunks, HD, W), BF16),
        pltpu.VMEM(pairs, BF16),
        pltpu.VMEM(pairs, BF16),
        pltpu.VMEM(mats, BF16),
        pltpu.VMEM(mats, BF16),
        pltpu.VMEM((2, n_y, MSG, W), BF16),
        pltpu.VMEM((2, MSG, W), BF16),
        pltpu.VMEM((2, n_x, MSG, W), BF16),
        pltpu.VMEM((2, MSG, W), BF16),
        pltpu.VMEM((n, 2 * T, T), F32),
        pltpu.VMEM((n, T, 2 * T), F32),
        pltpu.VMEM((2 * n, T), F32),
        pltpu.VMEM((n, T, 2 * T), F32),
        pltpu.VMEM(mats, F32),
        pltpu.VMEM((chunks, 4 * T, W), BF16),
        pltpu.VMEM((n, T, 2 * T), BF16),
        pltpu.VMEM(pairs, F32),
        pltpu.VMEM(pairs, F32),
        pltpu.VMEM((chunks, 2 * T, 4 * T), F32),
        pltpu.VMEM((chunks, chunks, 2 * T, 4 * T), BF16),
        pltpu.VMEM((2, n, 8, W), F32),
        pltpu.VMEM((2, n, HD, W), F32),
        pltpu.VMEM(pairs, F32),
        pltpu.VMEM(pairs, F32),
        pltpu.VMEM(pairs, F32),
        pltpu.SemaphoreType.DMA((3, n)),
        pltpu.SemaphoreType.DMA((3, n)),
        pltpu.SemaphoreType.DMA((5, n)),
        pltpu.SemaphoreType.DMA((5, n)),
        pltpu.SemaphoreType.DMA((2, n_y)),
        pltpu.SemaphoreType.DMA((2, n_y)),
        pltpu.SemaphoreType.DMA((2, n_x)),
        pltpu.SemaphoreType.DMA((2, n_x)),
        pltpu.SemaphoreType.DMA((2, chunks)),
        pltpu.SemaphoreType.DMA((2, chunks)),
        pltpu.SemaphoreType.DMA((2,)),
        pltpu.SemaphoreType.DMA((2,)),
        pltpu.SemaphoreType.DMA((6,)),
    ]
    sums = pl.pallas_call(
        functools.partial(kernel, n_ctx, n_y, n),
        out_shape=[jax.ShapeDtypeStruct(shape, BF16)] * 3,
        in_specs=[pl.BlockSpec(memory_space=pl.ANY)] * 6 + [vmem] + [pl.BlockSpec(memory_space=pltpu.SMEM)],
        out_specs=[vmem] * 3,
        scratch_shapes=scratch,
        compiler_params=pltpu.CompilerParams(
            collective_id=0, has_side_effects=True, vmem_limit_bytes=56 * 1024 * 1024
        ),
        name="span_backward",
    )(*args)
    return pl.pallas_call(
        scale_kernel,
        out_shape=[jax.ShapeDtypeStruct(shape, BF16)] * 3,
        in_specs=[vmem] * 3,
        out_specs=[vmem] * 3,
        name="scale_gradients",
    )(*sums)


def solution(mesh):
    tokens = P(("ctx", "head"), None)
    return jax.shard_map(
        functools.partial(body, mesh.shape["ctx"], mesh.shape["head"]),
        mesh=mesh,
        in_specs=(tokens,) * 7 + (P("ctx", None),),
        out_specs=(tokens,) * 3,
        check_vma=False,
    )
```

```python
import functools
import math

import jax
import jax.numpy as jnp
from jax import lax
from jax.experimental import pallas as pl
from jax.experimental.pallas import tpu as pltpu
from jax.sharding import PartitionSpec as P

T = 128
W = 128
HD = 64
MSG = 80
LOW = -1e30
F32 = jnp.float32
BF16 = jnp.bfloat16
MESH = pl.DeviceIdType.MESH


def dot(a, b, ca=1, cb=0):
    return lax.dot_general(a, b, (((ca,), (cb,)), ((), ())), preferred_element_type=F32)


def dot_split(a, b, ca=1, cb=0):
    high = a.astype(BF16)
    low = (a - high.astype(F32)).astype(BF16)
    return dot(high, b, ca, cb) + dot(low, b, ca, cb)


def halves(x):
    first = lax.broadcasted_iota(jnp.int32, x.shape, 1) < HD
    zero = jnp.zeros_like(x)
    return jnp.concatenate([jnp.where(first, x, zero), jnp.where(first, zero, x)], axis=0)


def fold(x):
    first = lax.broadcasted_iota(jnp.int32, (HD, W), 1) < HD
    return jnp.where(first, x[:HD], x[HD:])


def total_rows(total):
    high = total.astype(BF16).astype(F32)
    rest = total - high
    mid = rest.astype(BF16).astype(F32)
    low = rest - mid
    row = lax.broadcasted_iota(jnp.int32, (MSG - HD, W), 0)
    rows = jnp.where(row == 0, high, jnp.where(row == 1, mid, jnp.where(row == 2, low, 0.0)))
    return rows.astype(BF16)


def two_totals(first, second):
    upper, lower = total_rows(first), total_rows(second)
    return jnp.concatenate([upper[:8].astype(F32), lower[:8].astype(F32)], axis=0).astype(BF16)


def read_two(rows):
    rows = rows.astype(F32)
    return (
        jnp.sum(rows[:8], axis=0, keepdims=True),
        jnp.sum(rows[8:], axis=0, keepdims=True),
    )


def read_total(rows):
    return jnp.sum(rows.astype(F32), axis=0, keepdims=True)


def kernel(
    n_ctx,
    n_y,
    n,
    lq_hbm,
    lk_hbm,
    lv_hbm,
    sq_ref,
    sk_ref,
    up_ref,
    dec_ref,
    mask_ref,
    gq_ref,
    gk_ref,
    gv_ref,
    lq_ref,
    lk_ref,
    lv_ref,
    k_buf,
    q_buf,
    u_buf,
    lg_buf,
    lg_out,
    bs_mate,
    bs_out,
    cs_buf,
    cs_out,
    st_buf,
    st_out,
    mv_buf,
    mv_out,
    ri_buf,
    ri_out,
    row_buf,
    row_out,
    col_buf,
    col_out,
    weights,
    weights_t,
    level_rows,
    level_columns,
    reaches,
    u_wide,
    mixed,
    entries,
    leaving,
    scores,
    probs,
    loc_a,
    loc_b,
    acc_q,
    acc_k,
    acc_v,
    send_in,
    recv_in,
    send_mat,
    recv_mat,
    send_row,
    recv_row,
    send_col,
    recv_col,
    send_chip,
    recv_chip,
    send_mate,
    recv_mate,
    local_sem,
):
    here = lax.axis_index("ctx")
    me = lax.axis_index("head")
    n_x = n_ctx // n_y
    x, y = here // n_y, here % n_y
    chunks = n // 2
    chips = n // 2
    chip, core = me // 2, me % 2
    mate = me + 1 - 2 * core
    root_log2 = math.log2(math.e) / math.sqrt(HD)

    def peer_at(i):
        half = (i + 1) // 2
        odd = i % 2
        off = odd * half + (1 - odd) * (n - half)
        return (me + off) % n

    def lanes(p):
        return pl.ds(pl.multiple_of(p * W, W), W)

    def rounds(low, high, step, *carry):
        if carry:
            return lax.fori_loop(low, high, step, *carry)

        def plain(i, nothing):
            step(i)
            return nothing

        lax.fori_loop(low, high, plain, 0)

    def several(count, step, low=0, high=n):
        def turn(j):
            for q in range(count):
                step(count * j + q)

        rounds(low // count, high // count, turn)

    barrier = pltpu.get_barrier_semaphore()

    def greet_head(i):
        pl.semaphore_signal(
            barrier, inc=1, device_id=(here, (me + i) % n), device_id_type=MESH
        )

    def greet_ctx(k):
        pl.semaphore_signal(barrier, inc=1, device_id=(k, me), device_id_type=MESH)

    rounds(1, n, greet_head)
    rounds(1, n_y, lambda i: greet_ctx(x * n_y + (y + i) % n_y))
    rounds(1, n_x, lambda i: greet_ctx((x + i) % n_x * n_y + y))
    light = ((lq_hbm, lq_ref), (lk_hbm, lk_ref), (lv_hbm, lv_ref))
    light_copies = [
        pltpu.make_async_copy(src, dst, local_sem.at[3 + which])
        for which, (src, dst) in enumerate(light)
    ]
    for copy in light_copies:
        copy.start()
    pl.semaphore_wait(barrier, n - 1 + n_y - 1 + n_x - 1)

    def in_copy(which, src, buf, peer, slot):
        return pltpu.make_async_remote_copy(
            src_ref=src.at[:, lanes(peer)],
            dst_ref=buf.at[slot],
            send_sem=send_in.at[which, peer],
            recv_sem=recv_in.at[which, slot],
            device_id=(here, peer),
            device_id_type=MESH,
        )

    def mat_copy(which, src, buf, peer, slot):
        return pltpu.make_async_remote_copy(
            src_ref=src.at[peer],
            dst_ref=buf.at[slot],
            send_sem=send_mat.at[which, peer],
            recv_sem=recv_mat.at[which, slot],
            device_id=(here, peer),
            device_id_type=MESH,
        )

    def chip_copy(which, src, dst, peer, slot):
        return pltpu.make_async_remote_copy(
            src_ref=src,
            dst_ref=dst,
            send_sem=send_chip.at[which, peer],
            recv_sem=recv_chip.at[which, slot],
            device_id=(here, 2 * peer + core),
            device_id_type=MESH,
        )

    def sum_copy(peer, slot):
        return chip_copy(0, cs_out.at[peer], cs_buf.at[slot], peer, slot)

    def state_copy(peer, slot):
        return chip_copy(1, st_out.at[peer], st_buf.at[core, slot], peer, slot)

    def mate_copy(which, src, dst):
        return pltpu.make_async_remote_copy(
            src_ref=src,
            dst_ref=dst,
            send_sem=send_mate.at[which],
            recv_sem=recv_mate.at[which],
            device_id=(here, mate),
            device_id_type=MESH,
        )

    def chip_at(i):
        half = (i + 1) // 2
        odd = i % 2
        return (chip + odd * half + (1 - odd) * (chips - half)) % chips

    def row_copy(which, peer, slot):
        return pltpu.make_async_remote_copy(
            src_ref=row_out.at[which],
            dst_ref=row_buf.at[which, slot],
            send_sem=send_row.at[which, peer],
            recv_sem=recv_row.at[which, slot],
            device_id=(x * n_y + peer, me),
            device_id_type=MESH,
        )

    def col_copy(which, peer, slot):
        return pltpu.make_async_remote_copy(
            src_ref=col_out.at[which],
            dst_ref=col_buf.at[which, slot],
            send_sem=send_col.at[which, peer],
            recv_sem=recv_col.at[which, slot],
            device_id=(peer * n_y + y, me),
            device_id_type=MESH,
        )

    def pack(ref, a, s):
        ref[:HD] = s.astype(BF16)
        ref[HD:] = total_rows(a)

    def absorb(ref, carried):
        a, s = carried
        total = read_total(ref[HD:])
        return a * total, total * s + ref[:HD].astype(F32)

    def start_rows(which, a, s):
        pack(row_out.at[which], a, s)
        row_buf[which, y] = row_out[which]
        rounds(1, n_y, lambda i: row_copy(which, (y + i) % n_y, y).start())

    def fold_rows(which):
        def arrive(i):
            k = (y + i) % n_y
            row_copy(which, k, k).wait_recv()

        rounds(1, n_y, arrive)

        def step(i, carried):
            return absorb(row_buf.at[which, n_y - 1 - i if which else i], carried)

        mine = n_y - 1 - y if which else y
        part = rounds(0, mine, step, (one_a, zero_b))
        whole = rounds(mine, n_y, step, part)
        pack(col_out.at[which], *whole)
        low, high = (0, x) if which else (x + 1, n_x)
        rounds(low, high, lambda k: col_copy(which, k, x).start())
        return part

    def fold_columns(which, part):
        def step(i, carried):
            k = n_x - 1 - i if which else i
            col_copy(which, k, k).wait_recv()
            return absorb(col_buf.at[which, k], carried)

        other = rounds(0, n_x - 1 - x if which else x, step, (one_a, zero_b))
        return part[0] * other[1] + part[1]

    zero_b = jnp.zeros((HD, W), F32)
    one_a = jnp.ones((1, W), F32)
    inputs = ((sk_ref, k_buf), (sq_ref, q_buf), (up_ref, u_buf))
    for which, (src, buf) in enumerate(inputs):
        rounds(1, n, lambda i: in_copy(which, src, buf, peer_at(i), me).start())

    own_copies = [
        pltpu.make_async_copy(src.at[:, lanes(me)], buf.at[me], local_sem.at[which])
        for which, (src, buf) in enumerate(inputs)
    ]
    for copy in own_copies:
        copy.start()

    lower = lax.broadcasted_iota(jnp.int32, (T, T), 1) <= lax.broadcasted_iota(
        jnp.int32, (T, T), 0
    )
    tri = jnp.where(lower, 1.0, 0.0).astype(BF16)
    heads = dec_ref.shape[0]
    level_rows[...] = dot(dec_ref[...], tri, 1, 1)

    def level_up(p):
        pick = jnp.where(
            lax.broadcasted_iota(jnp.int32, (heads, 2 * T), 0)
            == 2 * p + lax.broadcasted_iota(jnp.int32, (heads, 2 * T), 1) // T,
            1.0,
            0.0,
        ).astype(BF16)
        level_columns[p] = dot(tri, dot(dec_ref[...], pick, 0, 0).astype(BF16))

    for p in range(n):
        level_up(p)

    for copy in light_copies:
        copy.wait()

    def prepare(i):
        p = peer_at(i)
        columns = [level_columns[p, :, h * T : (h + 1) * T] for h in range(2)]
        table = jnp.concatenate(
            [
                jnp.where(
                    lower,
                    jnp.exp(jnp.minimum(level_rows[pl.ds(2 * p + h, 1)] - columns[h], 0.0)),
                    0.0,
                )
                for h in range(2)
            ],
            axis=0,
        )
        table_t = jnp.concatenate([table[:T].T, table[T:].T], axis=1)
        weights[p] = table
        weights_t[p] = table_t
        first = lax.broadcasted_iota(jnp.int32, (T, W), 1) < HD
        level = jnp.where(first, columns[0], columns[1])
        last = level[T - 1 : T]
        enter = jnp.exp(-level)
        entries[p] = enter
        leave = jnp.exp(level - last)
        leaving[p] = leave
        lk = lk_ref[:, lanes(p)]
        lv = lv_ref[:, lanes(p)]
        lq = lq_ref[:, lanes(p)]
        sums = fold(dot_split(lk.astype(F32) * leave, lv, 0, 0))
        bs_out[p, :HD] = sums.astype(BF16)
        bs_out[p, HD:] = total_rows(jnp.exp(-last))

        mv_out[p] = (lq.astype(F32) * enter).T.astype(BF16)

        @pl.when(i > 0)
        def _():
            mat_copy(2, mv_out, mv_buf, p, me).start()

        mixed[p] = (dot(lk, halves(lq), 1, 1) * table_t).astype(BF16)

    rounds(0, n, prepare)
    mv_buf[me] = mv_out[me]
    sums_to_mate = mate_copy(0, bs_out, bs_mate)
    sums_to_mate.start()

    for which in range(2):
        src, buf = inputs[which]
        rounds(1, n, lambda i: in_copy(which, src, buf, peer_at(i), peer_at(i)).wait_recv())
        own_copies[which].wait()

    def soften(u):
        size = 2 * T
        wide = 2 * size
        both = jnp.concatenate([halves(q_buf[2 * u]), halves(q_buf[2 * u + 1])], axis=0)

        def bias(c, a, b):
            return (mask_ref[2 * u + b, 2 * c + a].astype(F32) - 1.0) * (-LOW)

        def peak(x):
            return jnp.max(x.reshape(T // 8, 8, size), axis=0)

        def score(c):
            keys = k_buf[pl.ds(2 * c, 2)].reshape(size, W)
            return dot(keys, both, 1, 1)

        def part(x, a, b):
            return x[a * T : (a + 1) * T, b * size : (b + 1) * size]

        def keep(c, parts):
            for a in range(2):
                for b in range(2):
                    scores[c, a * T : (a + 1) * T, b * size : (b + 1) * size] = parts[a][b]
            return jnp.concatenate(
                [jnp.maximum(peak(parts[0][b]), peak(parts[1][b])) for b in range(2)], axis=1
            )

        def first_pass(c, highest):
            x = score(c)
            parts = [[part(x, a, b) + bias(c, a, b) for b in range(2)] for a in range(2)]
            return jnp.maximum(highest, keep(c, parts))

        highest = rounds(0, u, first_pass, jnp.full((8, wide), LOW, F32))
        key = lax.broadcasted_iota(jnp.int32, (T, size), 0)
        query = lax.broadcasted_iota(jnp.int32, (T, size), 1) % T
        x = score(u)
        parts = [
            [
                jnp.where(key <= query, part(x, 0, 0) + bias(u, 0, 0), LOW),
                part(x, 0, 1) + bias(u, 0, 1),
            ],
            [
                jnp.full((T, size), LOW, F32),
                jnp.where(key <= query, part(x, 1, 1) + bias(u, 1, 1), LOW),
            ],
        ]
        highest = jnp.maximum(highest, keep(u, parts))
        highest = jnp.max(highest, axis=0, keepdims=True)

        def second_pass(c, total):
            e = jnp.exp2((scores[c] - highest) * root_log2)
            scores[c] = e
            return total + jnp.sum(e.reshape(size // 8, 8, wide), axis=0)

        total = rounds(0, u + 1, second_pass, jnp.zeros((8, wide), F32))
        inverse = 1.0 / jnp.sum(total, axis=0, keepdims=True)

        def third_pass(c):
            probs[c, u] = (scores[c] * inverse).astype(BF16)

        rounds(0, u + 1, third_pass)

    rounds(0, chunks, soften)

    sums_to_mate.wait_recv()

    def join(i):
        peer = chip_at(i)
        p = 2 * peer + core
        mine, other = bs_out[p, :HD].astype(F32), bs_mate[p, :HD].astype(F32)
        mine_a, other_a = read_total(bs_out[p, HD:]), read_total(bs_mate[p, HD:])
        early = jnp.where(core == 0, mine, other)
        late = jnp.where(core == 0, other, mine)
        early_a = jnp.where(core == 0, mine_a, other_a)
        late_a = jnp.where(core == 0, other_a, mine_a)
        cs_out[peer, :HD] = (late_a * early + late).astype(BF16)
        cs_out[peer, HD:] = two_totals(early_a, late_a)

        @pl.when(i > 0)
        def _():
            sum_copy(peer, chip).start()

    rounds(0, chips, join)
    cs_buf[chip] = cs_out[chip]

    rounds(1, n, lambda i: in_copy(2, up_ref, u_buf, peer_at(i), peer_at(i)).wait_recv())
    own_copies[2].wait()

    def widen(u):
        u_wide[u] = jnp.concatenate([halves(u_buf[2 * u]), halves(u_buf[2 * u + 1])], axis=0)

    rounds(0, chunks, widen)

    my_chunk = me // 2

    def light_pair(i):
        half = (i + 1) // 2
        odd = i % 2
        off = odd * half + (1 - odd) * (chunks - half)
        c = (my_chunk + off) % chunks

        def add(u, acc):
            return acc + dot(probs[c, u], u_wide[u])

        grad = rounds(c, chunks, add, jnp.zeros((2 * T, W), F32)).astype(BF16)
        lg_out[2 * c] = grad[:T]
        lg_out[2 * c + 1] = grad[T:]
        for side in range(2):

            @pl.when(2 * c + side != me)
            def _():
                mat_copy(1, lg_out, lg_buf, 2 * c + side, me).start()

    rounds(0, chunks, light_pair)
    lg_buf[me] = lg_out[me]

    rounds(1, n, lambda i: mat_copy(2, mv_out, mv_buf, peer_at(i), peer_at(i)).wait_recv())

    def reach(b):
        reaches[b] = fold(dot(mv_buf[b], lg_out[b]))

    several(4, reach)

    rounds(1, chips, lambda i: sum_copy(chip_at(i), chip_at(i)).wait_recv())

    def forward(c, carried):
        a, s = carried
        loc_a[0, c] = jnp.broadcast_to(a, (8, W))
        loc_b[0, c] = s
        early_a, late_a = read_two(cs_buf[c, HD:])
        total = early_a * late_a
        return a * total, total * s + cs_buf[c, :HD].astype(F32)

    start_rows(0, *rounds(0, chips, forward, (one_a, zero_b)))

    def backward(j, carried):
        c = chips - 1 - j
        totals = read_two(cs_buf[c, HD:])
        a, s = carried
        for side in (1, 0):
            loc_a[1, 2 * c + side] = jnp.broadcast_to(a, (8, W))
            loc_b[1, 2 * c + side] = s
            a, s = a * totals[side], totals[side] * s + reaches[2 * c + side]
        return a, s

    start_rows(1, *rounds(0, chips, backward, (one_a, zero_b)))

    part_in = fold_rows(0)
    part_back = fold_rows(1)
    span_in = fold_columns(0, part_in)

    def send_state(i):
        c = chip_at(i)
        st_out[c] = (loc_a[0, c, :1] * span_in + loc_b[0, c]).astype(BF16)

        @pl.when(i > 0)
        def _():
            state_copy(c, chip).start()

    rounds(0, chips, send_state)
    st_buf[core, chip] = st_out[chip]

    span_back = fold_columns(1, part_back)

    def send_reach(i):
        b = peer_at(i)
        ri_out[b] = (loc_a[1, b, :1] * span_back + loc_b[1, b]).astype(BF16)

        @pl.when(i > 0)
        def _():
            mat_copy(4, ri_out, ri_buf, b, me).start()

    several(2, send_reach)
    ri_buf[me] = ri_out[me]

    rounds(1, n, lambda i: mat_copy(1, lg_out, lg_buf, peer_at(i), peer_at(i)).wait_recv())

    def inside(p):
        lg2 = halves(lg_buf[p])
        lk = lk_ref[:, lanes(p)]
        lv = lv_ref[:, lanes(p)]
        lq = lq_ref[:, lanes(p)]
        back = (dot(lg2, lv, 1, 1) * weights[p]).astype(BF16)
        back_t = (dot(lv, lg2, 1, 1) * weights_t[p]).astype(BF16)
        wide = jnp.concatenate([back[:T], back[T:]], axis=1)
        acc_q[p] = dot(wide, halves(lk))
        acc_k[p] = dot(back_t, halves(lq))
        acc_v[p] = dot(mixed[p], lg2)

    several(2, inside, 0, n // 2)

    rounds(1, chips, lambda i: state_copy(chip_at(i), chip_at(i)).wait_recv())
    states_to_mate = mate_copy(1, st_buf.at[core], st_buf.at[core])
    states_to_mate.start()

    several(2, inside, n // 2, n)
    states_to_mate.wait_recv()

    def finish_query(p):
        state = st_buf[p % 2, p // 2].astype(F32)
        passed = read_total(bs_mate[p, HD:]) * state + bs_mate[p, :HD].astype(F32)
        state = jnp.where(core == 1, passed, state)
        high = state.astype(BF16)
        low = (state - high.astype(F32)).astype(BF16)
        lg = lg_buf[p]
        carried = dot(lg, halves(high), 1, 1) + dot(lg, halves(low), 1, 1)
        gq_ref[:, lanes(p)] = (acc_q[p] + entries[p] * carried).astype(BF16)

    several(2, finish_query)

    def finish(p):
        both = halves(ri_buf[p])
        leave = leaving[p]
        from_value = dot(lv_ref[:, lanes(p)], both, 1, 1)
        from_key = dot(lk_ref[:, lanes(p)], both)
        gk_ref[:, lanes(p)] = (acc_k[p] + leave * from_value).astype(BF16)
        gv_ref[:, lanes(p)] = (acc_v[p] + leave * from_key).astype(BF16)

    def finish_two(j):
        first, second = peer_at(2 * j), peer_at(2 * j + 1)

        @pl.when(j > 0)
        def _():
            mat_copy(4, ri_out, ri_buf, first, first).wait_recv()

        mat_copy(4, ri_out, ri_buf, second, second).wait_recv()
        finish(first)
        finish(second)

    rounds(0, n // 2, finish_two)

    def drain(i):
        p = peer_at(i)
        for which, (src, buf) in enumerate(inputs):
            in_copy(which, src, buf, p, me).wait_send()
        for which, src, buf in ((1, lg_out, lg_buf), (2, mv_out, mv_buf), (4, ri_out, ri_buf)):
            mat_copy(which, src, buf, p, me).wait_send()

    rounds(1, n, drain)

    def drain_chip(i):
        sum_copy(chip_at(i), chip).wait_send()
        state_copy(chip_at(i), chip).wait_send()

    rounds(1, chips, drain_chip)
    sums_to_mate.wait_send()
    states_to_mate.wait_send()
    for which in range(2):
        rounds(1, n_y, lambda i: row_copy(which, (y + i) % n_y, y).wait_send())
        low, high = (0, x) if which else (x + 1, n_x)
        rounds(low, high, lambda k: col_copy(which, k, x).wait_send())


def scale_kernel(*refs):
    scale = 1.0 / (HD * math.sqrt(HD))
    for src, dst in zip(refs[:3], refs[3:]):
        dst[...] = (src[...].astype(F32) * scale).astype(BF16)


def body(n_ctx, n, *args):
    shape = args[0].shape
    args = (*args[:6], args[6].T, args[7])
    vmem = pl.BlockSpec(memory_space=pltpu.VMEM)
    n_y = 8 if n_ctx % 8 == 0 else 2
    n_x = n_ctx // n_y
    chunks = n // 2
    pairs = (n, T, W)
    mats = (n, HD, W)
    scratch = [
        pltpu.VMEM(shape, BF16),
        pltpu.VMEM(shape, BF16),
        pltpu.VMEM(shape, BF16),
        pltpu.VMEM(pairs, BF16),
        pltpu.VMEM(pairs, BF16),
        pltpu.VMEM(pairs, BF16),
        pltpu.VMEM(pairs, BF16),
        pltpu.VMEM(pairs, BF16),
        pltpu.VMEM((n, MSG, W), BF16),
        pltpu.VMEM((n, MSG, W), BF16),
        pltpu.VMEM((chunks, MSG, W), BF16),
        pltpu.VMEM((chunks, MSG, W), BF16),
        pltpu.VMEM((2, chunks, HD, W), BF16),
        pltpu.VMEM((chunks, HD, W), BF16),
        pltpu.VMEM(pairs, BF16),
        pltpu.VMEM(pairs, BF16),
        pltpu.VMEM(mats, BF16),
        pltpu.VMEM(mats, BF16),
        pltpu.VMEM((2, n_y, MSG, W), BF16),
        pltpu.VMEM((2, MSG, W), BF16),
        pltpu.VMEM((2, n_x, MSG, W), BF16),
        pltpu.VMEM((2, MSG, W), BF16),
        pltpu.VMEM((n, 2 * T, T), F32),
        pltpu.VMEM((n, T, 2 * T), F32),
        pltpu.VMEM((2 * n, T), F32),
        pltpu.VMEM((n, T, 2 * T), F32),
        pltpu.VMEM(mats, F32),
        pltpu.VMEM((chunks, 4 * T, W), BF16),
        pltpu.VMEM((n, T, 2 * T), BF16),
        pltpu.VMEM(pairs, F32),
        pltpu.VMEM(pairs, F32),
        pltpu.VMEM((chunks, 2 * T, 4 * T), F32),
        pltpu.VMEM((chunks, chunks, 2 * T, 4 * T), BF16),
        pltpu.VMEM((2, n, 8, W), F32),
        pltpu.VMEM((2, n, HD, W), F32),
        pltpu.VMEM(pairs, F32),
        pltpu.VMEM(pairs, F32),
        pltpu.VMEM(pairs, F32),
        pltpu.SemaphoreType.DMA((3, n)),
        pltpu.SemaphoreType.DMA((3, n)),
        pltpu.SemaphoreType.DMA((5, n)),
        pltpu.SemaphoreType.DMA((5, n)),
        pltpu.SemaphoreType.DMA((2, n_y)),
        pltpu.SemaphoreType.DMA((2, n_y)),
        pltpu.SemaphoreType.DMA((2, n_x)),
        pltpu.SemaphoreType.DMA((2, n_x)),
        pltpu.SemaphoreType.DMA((2, chunks)),
        pltpu.SemaphoreType.DMA((2, chunks)),
        pltpu.SemaphoreType.DMA((2,)),
        pltpu.SemaphoreType.DMA((2,)),
        pltpu.SemaphoreType.DMA((6,)),
    ]
    rows = pl.BlockSpec((shape[0] // 4, shape[1]), lambda i: (i, 0))
    sums = pl.pallas_call(
        functools.partial(kernel, n_ctx, n_y, n),
        out_shape=[jax.ShapeDtypeStruct(shape, BF16)] * 3,
        in_specs=[pl.BlockSpec(memory_space=pl.ANY)] * 6 + [vmem] + [pl.BlockSpec(memory_space=pltpu.SMEM)],
        out_specs=[vmem] * 3,
        scratch_shapes=scratch,
        compiler_params=pltpu.CompilerParams(
            collective_id=0, has_side_effects=True, vmem_limit_bytes=56 * 1024 * 1024
        ),
        name="span_backward",
    )(*args)
    return pl.pallas_call(
        scale_kernel,
        out_shape=[jax.ShapeDtypeStruct(shape, BF16)] * 3,
        grid=(4,),
        in_specs=[rows] * 3,
        out_specs=[rows] * 3,
        name="scale_gradients",
    )(*sums)


def solution(mesh):
    tokens = P(("ctx", "head"), None)
    return jax.shard_map(
        functools.partial(body, mesh.shape["ctx"], mesh.shape["head"]),
        mesh=mesh,
        in_specs=(tokens,) * 7 + (P("ctx", None),),
        out_specs=(tokens,) * 3,
        check_vma=False,
    )
```
